256 devices in a mesh: gx: 16 (over x, y), gy: 16 (over z, core).
Axes of the slice: x: 4, y: 4, z: 8, core: 2. Of those that a mesh axis runs over, the one named last changes fastest.
Arguments:
- snapshots: bfloat16 [3, 1024, 1024, 256], P(None, 'gx', 'gy'), may hold values from -70 to 70
- prior: float32 [256, 256], replicated, may hold values from -0.15 to 0.5, as said below
Outputs:
- modes: float32 [3, 512, 512, 256], P(None, 'gx', 'gy')
- factor: float32 [256, 256], replicated
The draws below stay inside these ranges and needn't reach their ends.
Inputs may be any that keep to these rules, and one draw needn't show every extreme that they name: `prior`: upper triangular with a positive diagonal.
All inputs are finite; a program needn't handle non-finite values.
Results may differ from the reference program's by a relative error of at most 0.008.
Values may be sent and summed in bfloat16 or wider, within the bound.
A program may use at most 320 MiB of HBM per device.

```python
import jax
import jax.numpy as jnp
from jax import lax

K = 256
NX = 1024
NY = 1024


def draw_snapshots(key, part):
    key = jax.random.fold_in(key, 11)
    key_values, key_column, key_rough = jax.random.split(key, 3)
    column = jnp.exp(jnp.log(10.0) * (jax.random.uniform(key_column, (K,)) - 0.5))
    xcoord = jnp.arange(NX, dtype=jnp.float32) / NX - 0.5
    ycoord = jnp.arange(NY, dtype=jnp.float32) / NY - 0.5
    ramp = jnp.exp(jnp.log(3.0) * (xcoord[:, None] + ycoord[None, :]))
    rough = jnp.exp(jnp.log(3.0) * (jax.random.uniform(key_rough, (3, NX, NY)) - 0.5))
    base = jnp.clip(jax.random.normal(key_values, (3, NX, NY, K)), -4.0, 4.0)
    scaled = base * (ramp[None, :, :] * rough)[..., None] * column
    return scaled.astype(jnp.bfloat16)


def draw_prior(key, part):
    key = jax.random.fold_in(key, 23)
    key_diag, key_upper = jax.random.split(key, 2)
    diagonal = jnp.exp(jax.random.uniform(key_diag, (K,), minval=jnp.log(0.1), maxval=jnp.log(0.5)))
    upper = jnp.clip(0.03 * jax.random.normal(key_upper, (K, K)), -0.15, 0.15)
    return (jnp.triu(upper, 1) + jnp.diag(diagonal)).astype(jnp.float32)


def setup_inputs(seed: int = 0) -> dict:
    seeds = jax.random.split(jax.random.key(seed), 3)
    return {
        "snapshots": draw_snapshots(jax.random.fold_in(seeds[2], 71), 0),
        "prior": draw_prior(jax.random.fold_in(seeds[2], 71), 0),
    }


filter_taps = (1.0 / 256, 8.0 / 256, 28.0 / 256, 56.0 / 256, 70.0 / 256, 56.0 / 256, 28.0 / 256, 8.0 / 256, 1.0 / 256)

def coarsen(values_in, along):
    length = values_in.shape[along]
    result = None
    for offset in range(9):
        shifted = jnp.roll(values_in, 4 - offset, axis=along)
        picked = lax.slice_in_dim(shifted, 0, length, 2, along).astype(jnp.float32)
        term = filter_taps[offset] * picked
        result = term if result is None else result + term
    return result

def filter_one(component):
    rough = lax.optimization_barrier(coarsen(component, 1).astype(jnp.bfloat16))
    return coarsen(rough, 0)

def reference(snapshots, prior):
    coarse = lax.map(filter_one, snapshots)
    coarse_rows = coarse.reshape(-1, K)
    row_count = coarse_rows.shape[0]
    gram_total = jnp.dot(coarse_rows.T, coarse_rows, precision=lax.Precision.HIGHEST) / row_count
    gram_total = gram_total + jnp.dot(prior.T, prior, precision=lax.Precision.HIGHEST)
    lower_factor = jnp.linalg.cholesky(gram_total)
    solved = jax.scipy.linalg.solve_triangular(lower_factor, coarse_rows.T, lower=True)
    modes = solved.T.reshape(coarse.shape)
    return (modes, lower_factor.T)
```

```python
import jax
import jax.numpy as jnp
from jax import lax
from jax.experimental import pallas as pl
from jax.experimental.pallas import tpu as pltpu
from jax.sharding import PartitionSpec as P

f32 = jnp.float32
bf16 = jnp.bfloat16
MESH = pl.DeviceIdType.MESH
TAPS = (1, 8, 28, 56, 70, 56, 28, 8, 1)
RING = 16
PARTS = 3
FINE = 64
HALF = 32
K = 256
LANES = 128
ROWS = 40
GROUP = 4
SLOTS = 40
CHUNK = 24
PANEL = 16


def y_matrix():
    shape = (GROUP * ROWS, GROUP * FINE)
    row = lax.broadcasted_iota(jnp.int32, shape, 0)
    column = lax.broadcasted_iota(jnp.int32, shape, 1)
    slab = row // ROWS
    index = row % ROWS
    cell = jnp.where(index < HALF, index, jnp.where(index < HALF + 2, index - HALF - 2, index - 2))
    offset = column % FINE - 2 * cell + 4
    offset = jnp.where((slab == column // FINE) & (index < HALF + 4), offset, -1)
    taps = jnp.zeros(shape, f32)
    for place, tap in enumerate(TAPS):
        taps = jnp.where(offset == place, tap / 65536.0, taps)
    return jnp.where(slab % 2 == 1, 8.0 * taps, taps).astype(bf16)


def x_sum(load, cell):
    total = None

    def pair(first, second, low, high):
        have = [load(2 * q + second) for q in (low, high) if 0 <= q < HALF]
        if not have:
            return None
        value = have[0] if len(have) == 1 else have[0] + have[1]
        return value if first == 1.0 else first * value

    terms = [
        pair(1.0, 0, cell - 2, cell + 2),
        pair(28.0, 0, cell - 1, cell + 1),
        pair(70.0, 0, cell, -1),
        pair(1.0, 1, cell - 2, cell + 1),
        pair(7.0, 1, cell - 1, cell),
    ]
    for term in terms:
        if term is not None:
            total = term if total is None else total + term
    return total


def filter_kernel(
    snap_ref,
    prior_ref,
    coarse_ref,
    gram_ref,
    tile,
    prior_tile,
    ysum,
    edge,
    coarse,
    rounded,
    x_out,
    x_in,
    y_out,
    y_in,
    c_out,
    c_in,
    packed,
    prior_gram,
    rs_in,
    gy_in,
    ag_in,
    load_sem,
    store_sem,
    halo_send,
    halo_recv,
    rs_send,
    rs_recv,
    gy_send,
    gy_recv,
    ag_send,
    ag_recv,
):
    gx = lax.axis_index("gx")
    gy = lax.axis_index("gy")
    gx_next, gx_last = lax.rem(gx + 1, RING), lax.rem(gx + RING - 1, RING)
    gy_next, gy_last = lax.rem(gy + 1, RING), lax.rem(gy + RING - 1, RING)

    slabs = 16
    loads = []
    for m in range(PARTS):
        for q in range(FINE // slabs):
            place = (m, pl.ds(q * slabs, slabs))
            loads.append(
                pltpu.make_async_copy(
                    snap_ref.at[place], tile.at[place], load_sem.at[len(loads)]
                )
            )
    load_prior = pltpu.make_async_copy(prior_ref, prior_tile, load_sem.at[len(loads)])
    for load in loads:
        load.start()
    load_prior.start()

    barrier = pltpu.get_barrier_semaphore()

    def greet(step, carry):
        pl.semaphore_signal(
            barrier, inc=1, device_id=(lax.rem(gx + step, RING), gy), device_id_type=MESH
        )
        pl.semaphore_signal(
            barrier, inc=1, device_id=(gx, lax.rem(gy + step, RING)), device_id_type=MESH
        )
        return carry

    lax.fori_loop(1, RING, greet, 0)
    for ox in (gx_last, gx_next):
        for oy in (gy_last, gy_next):
            pl.semaphore_signal(barrier, inc=1, device_id=(ox, oy), device_id_type=MESH)

    taps = y_matrix()
    for m in range(PARTS):
        for q in range(FINE // slabs):
            loads[m * (FINE // slabs) + q].wait()

            def y_group(g, carry, m=m, q=q):
                first = q * slabs + g * GROUP
                fine = tile[m, pl.ds(first, GROUP)].reshape(GROUP * FINE, K)
                sums = jnp.dot(taps, fine, preferred_element_type=f32)
                ysum[m, pl.ds(first, GROUP)] = sums.reshape(GROUP, ROWS, K)
                return carry

            lax.fori_loop(0, slabs // GROUP, y_group, 0, unroll=True)

    for m in range(PARTS):
        for side in range(2):
            for step in range(2):
                cell = (-2, HALF)[side] + step
                value = x_sum(lambda x: ysum[m, x, pl.ds(0, HALF), :], cell)
                x_out[side, m, step] = value.astype(bf16)

    def edge_part(m, carry):
        for slot in range(HALF + 4):
            cell = slot if slot < HALF else (slot - HALF - 2 if slot < HALF + 2 else slot - 2)
            value = x_sum(lambda x: ysum[m, x, pl.ds(HALF, 8), :], cell)
            rows = pl.ds(pl.multiple_of(m * (SLOTS * 8) + slot * 8, 8), 8)
            edge[0, rows, :] = value[:, :LANES]
            edge[1, rows, :] = value[:, LANES:]
        for slot in range(HALF + 4, SLOTS):
            rows = pl.ds(pl.multiple_of(m * (SLOTS * 8) + slot * 8, 8), 8)
            edge[:, rows, :] = jnp.zeros((2, 8, LANES), f32)
        return carry

    pl.semaphore_wait(barrier, 2 * (RING - 1) + 4)
    halos = []

    def send(source, target, peer):
        copy = pltpu.make_async_remote_copy(
            src_ref=source,
            dst_ref=target,
            send_sem=halo_send.at[len(halos)],
            recv_sem=halo_recv.at[len(halos)],
            device_id=peer,
            device_id_type=MESH,
        )
        copy.start()
        halos.append(copy)

    send(x_out.at[0], x_in.at[0], (gx_last, gy))
    send(x_out.at[1], x_in.at[1], (gx_next, gy))

    lax.fori_loop(0, PARTS, edge_part, 0)
    for side in range(2):
        for m in range(PARTS):
            outer = []
            for step in range(2):
                start = m * SLOTS * 8 + side * 2 + step
                picked = jnp.concatenate(
                    [edge[h, pl.ds(start, SLOTS, stride=8), :] for h in range(2)], axis=1
                )
                y_out[side, m, step] = picked[:HALF].astype(bf16)
                outer.append(picked[HALF:])
            c_out[side, pl.ds(m * 16, 16), :] = jnp.concatenate(outer, axis=0).astype(bf16)
    send(y_out.at[0], y_in.at[0], (gx, gy_last))
    send(y_out.at[1], y_in.at[1], (gx, gy_next))
    for side, oy in ((0, gy_last), (1, gy_next)):
        for other, ox in ((0, gx_last), (1, gx_next)):
            send(c_out.at[side], c_in.at[side, other], (ox, oy))

    def inside(step, carry):
        m = step // 4
        row = pl.multiple_of(lax.rem(step, 4) * 8, 8)
        for cell in range(HALF):
            value = x_sum(lambda x: ysum[m, x, pl.ds(row, 8), :], cell)
            rows = pl.ds(pl.multiple_of(m * (HALF * HALF) + cell * HALF + row, 8), 8)
            coarse[0, rows, :] = value[:, :LANES]
            coarse[1, rows, :] = value[:, LANES:]
        return carry

    lax.fori_loop(0, PARTS * 4, inside, 0)

    load_prior.wait()
    half = K // 2
    squared = lax.dot_general(
        prior_tile[...],
        prior_tile[...],
        (((0,), (0,)), ((), ())),
        precision=lax.Precision.HIGHEST,
        preferred_element_type=f32,
    )
    prior_gram[0:half, :] = squared[:half, :half]
    prior_gram[half:K, :] = squared[:half, half:]
    prior_gram[K : K + half, :] = squared[half:, half:]

    for copy in halos:
        copy.wait()
    for m in range(PARTS):
        for side in range(2):
            for step in range(2):
                cell = (HALF - 2, 0)[side] + step
                rows = pl.ds(m * HALF * HALF + cell * HALF, HALF)
                value = x_in[side, m, step].astype(f32)
                for h in range(2):
                    coarse[h, rows, :] += value[:, h * LANES : (h + 1) * LANES]
    for m in range(PARTS):
        for side in range(2):
            for step in range(2):
                cell = (HALF - 2, 0)[side] + step
                rows = pl.ds(m * HALF * HALF + cell, HALF, stride=HALF)
                value = y_in[side, m, step].astype(f32)
                for h in range(2):
                    coarse[h, rows, :] += value[:, h * LANES : (h + 1) * LANES]
    for side in range(2):
        for other in range(2):
            corner = c_in[side, other].astype(f32)
            for m in range(PARTS):
                for step in range(2):
                    column = (HALF - 2, 0)[side] + step
                    for along in range(2):
                        row = (HALF - 2, 0)[other] + along
                        source = (m * 2 + step) * 8 + other * 2 + along
                        target = m * HALF * HALF + row * HALF + column
                        value = corner[source : source + 1, :]
                        for h in range(2):
                            lanes = value[:, h * LANES : (h + 1) * LANES]
                            coarse[h, target : target + 1, :] += lanes

    packed[...] = jnp.zeros(packed.shape, f32)
    block = 512

    def cross(step, carry):
        rows = pl.ds(pl.multiple_of(step * block, block), block)
        part = jnp.concatenate([coarse[h, rows, :] for h in range(2)], axis=1).astype(bf16)
        rounded[rows, :] = part
        contract = (((0,), (0,)), ((), ()))
        top = lax.dot_general(part[:, :half], part, contract, preferred_element_type=f32)
        low = lax.dot_general(part[:, half:], part[:, half:], contract, preferred_element_type=f32)
        sums = jnp.concatenate([top[:, :half], top[:, half:], low], axis=0)
        packed[...] += sums.reshape(packed.shape)
        return carry

    lax.fori_loop(0, PARTS * HALF * HALF // block, cross, 0)
    store = pltpu.make_async_copy(rounded, coarse_ref, store_sem)
    store.start()

    def exchange(source_of, target, send_sem, recv_sem, along, me):
        copies = []
        for step in range(1, RING):
            peer = lax.rem(me + step, RING)
            copies.append(
                pltpu.make_async_remote_copy(
                    src_ref=source_of(peer),
                    dst_ref=target.at[me],
                    send_sem=send_sem.at[step],
                    recv_sem=recv_sem.at[step],
                    device_id=(peer, gy) if along == 0 else (gx, peer),
                    device_id_type=MESH,
                )
            )
        for copy in copies:
            copy.start()
        for copy in copies:
            copy.wait()

    def sum_slots(slots):
        total = slots[0]
        for slot in range(1, RING):
            total = total + slots[slot]
        return total

    rs_in[gx] = packed[gx]
    exchange(lambda peer: packed.at[peer], rs_in, rs_send, rs_recv, 0, gx)
    gy_in[gy] = sum_slots(rs_in)
    exchange(lambda peer: gy_in.at[gy], gy_in, gy_send, gy_recv, 1, gy)
    ag_in[gx] = sum_slots(gy_in)
    exchange(lambda peer: ag_in.at[gx], ag_in, ag_send, ag_recv, 0, gx)

    count = PARTS * HALF * HALF * RING * RING
    gram_ref[...] = ag_in[...].reshape(gram_ref.shape) * (1.0 / count) + prior_gram[...]
    store.wait()


def filter_call(snapshots, prior):
    rows = PARTS * HALF * HALF
    vmem = pltpu.VMEM
    dma = pltpu.SemaphoreType.DMA
    return pl.pallas_call(
        filter_kernel,
        out_shape=(
            jax.ShapeDtypeStruct((rows, K), bf16),
            jax.ShapeDtypeStruct((K + K // 2, K // 2), f32),
        ),
        in_specs=[pl.BlockSpec(memory_space=pl.ANY)] * 2,
        out_specs=(pl.BlockSpec(memory_space=pl.ANY), pl.BlockSpec(memory_space=pltpu.VMEM)),
        scratch_shapes=[
            vmem((PARTS, FINE, FINE, K), bf16),
            vmem((K, K), f32),
            vmem((PARTS, FINE, ROWS, K), f32),
            vmem((2, PARTS * SLOTS * 8, LANES), f32),
            vmem((2, rows, LANES), f32),
            vmem((rows, K), bf16),
            vmem((2, PARTS, 2, HALF, K), bf16),
            vmem((2, PARTS, 2, HALF, K), bf16),
            vmem((2, PARTS, 2, HALF, K), bf16),
            vmem((2, PARTS, 2, HALF, K), bf16),
            vmem((2, PARTS * 16, K), bf16),
            vmem((2, 2, PARTS * 16, K), bf16),
            vmem((RING, CHUNK, K // 2), f32),
            vmem((K + K // 2, K // 2), f32),
            vmem((RING, CHUNK, K // 2), f32),
            vmem((RING, CHUNK, K // 2), f32),
            vmem((RING, CHUNK, K // 2), f32),
            dma((13,)),
            dma,
            dma((8,)),
            dma((8,)),
            dma((RING,)),
            dma((RING,)),
            dma((RING,)),
            dma((RING,)),
            dma((RING,)),
            dma((RING,)),
        ],
        compiler_params=pltpu.CompilerParams(
            collective_id=0, has_side_effects=True, vmem_limit_bytes=48 * 2**20
        ),
        name="filter_and_gram",
    )(snapshots, prior)


def split(value):
    high = value.astype(bf16)
    rest = value - high.astype(f32)
    middle = rest.astype(bf16)
    return high, middle, (rest - middle.astype(f32)).astype(bf16)


def factor_panels(work, upper, inverse):
    below = lax.broadcasted_iota(jnp.int32, (PANEL, 128), 0)
    for first in range(0, K, PANEL):
        rows = pl.ds(first, PANEL)
        strip = work[rows, :]
        columns = [
            jnp.broadcast_to(strip[:, first + k : first + k + 1], (PANEL, 128))
            for k in range(PANEL)
        ]
        tiles = [strip[:, t : t + 128] for t in range(0, 2 * K, 128)]
        pivots = jnp.zeros((PANEL, 128), f32)
        for j in range(PANEL):
            pivot = jnp.broadcast_to(columns[j][j : j + 1, :], (PANEL, 128))
            pivots = jnp.where(below == j, pivot, pivots)
            if j == PANEL - 1:
                break
            factor = jnp.where(below > j, columns[j] / pivot, 0.0)
            for k in range(j + 1, PANEL):
                columns[k] -= factor * jnp.broadcast_to(columns[k][j : j + 1, :], (PANEL, 128))
            tiles = [t - factor * jnp.broadcast_to(t[j : j + 1, :], (PANEL, 128)) for t in tiles]
        scale = lax.rsqrt(pivots)
        strip = jnp.concatenate([t * scale for t in tiles], axis=1)
        upper[rows, :] = strip[:, :K]
        inverse[rows, :] = strip[:, K:]
        done = first + PANEL
        if done < K:
            high, middle, low = split(strip)
            left = jnp.concatenate([high, high, middle, high, low, middle], axis=0)
            right = jnp.concatenate([high, middle, high, low, high, middle], axis=0)
            work[done:, :] -= lax.dot_general(
                left[:, done:K], right, (((0,), (0,)), ((), ())), preferred_element_type=f32
            )


def factor_kernel(
    coarse_ref, gram_ref, modes_ref, upper_ref, rows_in, work, upper, inverse, out, load_sem, store_sem
):
    load = pltpu.make_async_copy(coarse_ref, rows_in, load_sem)
    load.start()
    row = lax.broadcasted_iota(jnp.int32, (K, K), 0)
    column = lax.broadcasted_iota(jnp.int32, (K, K), 1)
    half = K // 2
    work[:half, :half] = gram_ref[:half, :]
    work[:half, half:K] = gram_ref[half:K, :]
    work[half:, :half] = jnp.zeros((half, half), f32)
    work[half:, half:K] = gram_ref[K:, :]
    work[:, K:] = jnp.where(row == column, 1.0, 0.0)
    factor_panels(work, upper, inverse)
    upper_ref[...] = jnp.where(row <= column, upper[...], 0.0)
    high, middle, low = split(inverse[...].T)
    load.wait()
    count = rows_in.shape[0]
    block = 512
    stores = []
    for step in range(count // block):
        rows = pl.ds(step * block, block)
        part = rows_in[rows, :]
        value = jnp.dot(part, high, preferred_element_type=f32)
        value += jnp.dot(part, middle, preferred_element_type=f32)
        out[rows, :] = value
        stores.append(
            pltpu.make_async_copy(out.at[rows], modes_ref.at[rows], store_sem.at[step])
        )
        stores[-1].start()
    for store in stores:
        store.wait()


def factor_call(coarse, gram):
    rows = coarse.shape[0]
    vmem = pltpu.VMEM
    return pl.pallas_call(
        factor_kernel,
        out_shape=(jax.ShapeDtypeStruct((rows, K), f32), jax.ShapeDtypeStruct((K, K), f32)),
        in_specs=[pl.BlockSpec(memory_space=pl.ANY), pl.BlockSpec(memory_space=pltpu.VMEM)],
        out_specs=(pl.BlockSpec(memory_space=pl.ANY), pl.BlockSpec(memory_space=pltpu.VMEM)),
        scratch_shapes=[
            vmem((rows, K), bf16),
            vmem((K, 2 * K), f32),
            vmem((K, K), f32),
            vmem((K, K), f32),
            vmem((rows, K), f32),
            pltpu.SemaphoreType.DMA,
            pltpu.SemaphoreType.DMA((rows // 512,)),
        ],
        compiler_params=pltpu.CompilerParams(vmem_limit_bytes=48 * 2**20),
        name="factor_and_modes",
    )(coarse, gram)


def shards(snapshots, prior):
    coarse, gram = filter_call(snapshots, prior)
    modes, upper = factor_call(coarse, gram)
    return (modes.reshape(PARTS, HALF, HALF, K), upper)


def solution(mesh):
    return jax.shard_map(
        shards,
        mesh=mesh,
        in_specs=(P(None, "gx", "gy", None), P()),
        out_specs=(P(None, "gx", "gy", None), P()),
        check_vma=False,
    )
```

```python
import jax
import jax.numpy as jnp
from jax import lax
from jax.experimental import pallas as pl
from jax.experimental.pallas import tpu as pltpu
from jax.sharding import PartitionSpec as P

f32 = jnp.float32
bf16 = jnp.bfloat16
MESH = pl.DeviceIdType.MESH
TAPS = (1, 8, 28, 56, 70, 56, 28, 8, 1)
RING = 16
PARTS = 3
FINE = 64
HALF = 32
K = 256
LANES = 128
ROWS = 40
GROUP = 4
SLOTS = 40
DEEP = 8
MEMBERS = 32
PANEL = 16


def y_matrix():
    shape = (GROUP * ROWS, GROUP * FINE)
    row = lax.broadcasted_iota(jnp.int32, shape, 0)
    column = lax.broadcasted_iota(jnp.int32, shape, 1)
    slab = row // ROWS
    index = row % ROWS
    cell = jnp.where(index < HALF, index, jnp.where(index < HALF + 2, index - HALF - 2, index - 2))
    offset = column % FINE - 2 * cell + 4
    offset = jnp.where((slab == column // FINE) & (index < HALF + 4), offset, -1)
    taps = jnp.zeros(shape, f32)
    for place, tap in enumerate(TAPS):
        taps = jnp.where(offset == place, tap / 65536.0, taps)
    return jnp.where(slab % 2 == 1, 8.0 * taps, taps).astype(bf16)


def x_sum(load, cell):
    total = None

    def pair(first, second, low, high):
        have = [load(2 * q + second) for q in (low, high) if 0 <= q < HALF]
        if not have:
            return None
        value = have[0] if len(have) == 1 else have[0] + have[1]
        return value if first == 1.0 else first * value

    terms = [
        pair(1.0, 0, cell - 2, cell + 2),
        pair(28.0, 0, cell - 1, cell + 1),
        pair(70.0, 0, cell, -1),
        pair(1.0, 1, cell - 2, cell + 1),
        pair(7.0, 1, cell - 1, cell),
    ]
    for term in terms:
        if term is not None:
            total = term if total is None else total + term
    return total


def x_cell(slot):
    return slot if slot < HALF else (slot - HALF - 2 if slot < HALF + 2 else slot - 2)


def cross(left, right):
    contract = (((0,), (0,)), ((), ()))
    return lax.dot_general(left, right, contract, preferred_element_type=f32)


def cross_blocks(part):
    top = cross(part[:, :LANES], part)
    return jnp.stack([top[:, :LANES], top[:, LANES:], cross(part[:, LANES:], part[:, LANES:])])


def pack(low, mixed, high):
    row = lax.broadcasted_iota(jnp.int32, (LANES, LANES), 0)
    column = lax.broadcasted_iota(jnp.int32, (LANES, LANES), 1)
    shared = jnp.where(row <= column, low, high)
    diagonal = jnp.sum(jnp.where(row == column, high, 0.0), axis=0, keepdims=True)
    return mixed, shared, diagonal


def filter_kernel(
    snap_ref,
    prior_ref,
    coarse_ref,
    gram_ref,
    tile,
    prior_tile,
    ysum,
    edge,
    coarse,
    rounded,
    border,
    x_out,
    x_in,
    y_out,
    y_in,
    c_stage,
    c_out,
    c_in,
    blocks,
    packed,
    prior_gram,
    rs_in,
    z_in,
    ag_in,
    load_sem,
    store_sem,
    halo_send,
    halo_recv,
    rs_send,
    rs_recv,
    z_send,
    z_recv,
    ag_send,
    ag_recv,
):
    gx = lax.axis_index("gx")
    gy = lax.axis_index("gy")
    core = lax.rem(gy, 2)
    zed = gy // 2
    gx_next, gx_last = lax.rem(gx + 1, RING), lax.rem(gx + RING - 1, RING)
    gy_next, gy_last = lax.rem(gy + 1, RING), lax.rem(gy + RING - 1, RING)

    slabs = 16
    loads = []
    for m in range(PARTS):
        for q in range(FINE // slabs):
            place = (m, pl.ds(q * slabs, slabs))
            loads.append(
                pltpu.make_async_copy(
                    snap_ref.at[place], tile.at[place], load_sem.at[len(loads)]
                )
            )
    load_prior = pltpu.make_async_copy(prior_ref, prior_tile, load_sem.at[len(loads)])
    for load in loads:
        load.start()
    load_prior.start()

    barrier = pltpu.get_barrier_semaphore()

    def greet(peer):
        pl.semaphore_signal(barrier, inc=1, device_id=peer, device_id_type=MESH)

    def greet_z(step, carry):
        greet((gx, 2 * lax.rem(zed + step, DEEP) + core))
        return carry

    def greet_member(step, carry):
        other = lax.rem(gx * 2 + core + step, MEMBERS)
        greet((other // 2, 2 * zed + lax.rem(other, 2)))
        return carry

    lax.fori_loop(1, DEEP, greet_z, 0)
    lax.fori_loop(1, MEMBERS, greet_member, 0)
    for oy in (gy_last, gy_next):
        for ox in (gx_last, gx, gx_next):
            greet((ox, oy))
    for ox in (gx_last, gx_next):
        greet((ox, gy))

    halos = []

    def send(source, target, peer):
        copy = pltpu.make_async_remote_copy(
            src_ref=source,
            dst_ref=target,
            send_sem=halo_send.at[len(halos)],
            recv_sem=halo_recv.at[len(halos)],
            device_id=peer,
            device_id_type=MESH,
        )
        copy.start()
        halos.append(copy)

    c_stage[:, :, :, 8:, :] = jnp.zeros((2, 2, 2, 8, LANES), f32)
    taps = y_matrix()
    for m in range(PARTS):
        for q in range(FINE // slabs):
            loads[m * (FINE // slabs) + q].wait()
            for g in range(slabs // GROUP):
                first = q * slabs + g * GROUP
                fine = tile[m, pl.ds(first, GROUP)].reshape(GROUP * FINE, K)
                sums = jnp.dot(taps, fine, preferred_element_type=f32)
                ysum[m, pl.ds(first, GROUP)] = sums.reshape(GROUP, ROWS, K)

        for side in range(2):
            for step in range(2):
                cell = (-2, HALF)[side] + step
                value = x_sum(lambda x: ysum[m, x, pl.ds(0, HALF), :], cell)
                x_out[side, m, step] = value.astype(bf16)

        for slot in range(HALF + 4):
            value = x_sum(lambda x: ysum[m, x, pl.ds(HALF, 8), :], x_cell(slot))
            rows = pl.ds(m * (SLOTS * 8) + slot * 8, 8)
            edge[0, rows, :] = value[:, :LANES]
            edge[1, rows, :] = value[:, LANES:]
        for side in range(2):
            for step in range(2):
                start = m * SLOTS * 8 + side * 2 + step
                picked = [edge[h, pl.ds(start, HALF, stride=8), :] for h in range(2)]
                y_out[side, m, step] = jnp.concatenate(picked, axis=1).astype(bf16)
            for other in range(2):
                for along in range(2):
                    start = m * SLOTS * 8 + (HALF + other * 2 + along) * 8 + side * 2
                    for h in range(2):
                        c_stage[h, side, other, pl.ds((m * 2 + along) * 2, 2), :] = edge[
                            h, pl.ds(start, 2), :
                        ]

        if m >= 1:
            if m == 1:
                pl.semaphore_wait(barrier, DEEP - 1 + MEMBERS - 1 + 8)
            for part in (0, 1) if m == 1 else (m,):
                send(x_out.at[0, part], x_in.at[0, part], (gx_last, gy))
                send(x_out.at[1, part], x_in.at[1, part], (gx_next, gy))
                send(y_out.at[0, part], y_in.at[0, part], (gx, gy_last))
                send(y_out.at[1, part], y_in.at[1, part], (gx, gy_next))

    for side, oy in ((0, gy_last), (1, gy_next)):
        for other, ox in ((0, gx_last), (1, gx_next)):
            corner = [c_stage[h, side, other] for h in range(2)]
            c_out[side, other] = jnp.concatenate(corner, axis=1).astype(bf16)
            send(c_out.at[side, other], c_in.at[side, other], (ox, oy))

    along_y = lax.broadcasted_iota(jnp.int32, (16, LANES), 0)

    def inside(step, carry):
        m = step // 2
        row = pl.multiple_of(lax.rem(step, 2) * 16, 16)
        y = along_y + row
        kept = (y >= 2) & (y < HALF - 2)
        for h in range(2):
            lanes = pl.ds(h * LANES, LANES)
            for cell in range(HALF):
                value = x_sum(lambda x: ysum[m, x, pl.ds(row, 16), lanes], cell)
                rows = pl.ds(pl.multiple_of(m * (HALF * HALF) + cell * HALF + row, 16), 16)
                coarse[h, rows, :] = value
                rounded[rows, lanes] = jnp.where(kept, value, 0.0).astype(bf16)
        return carry

    lax.fori_loop(0, PARTS * 2, inside, 0)

    blocks[...] = jnp.zeros(blocks.shape, f32)
    size = (HALF - 4) * HALF // 2

    def cross_inside(step, carry):
        start = (step // 2) * HALF * HALF + 2 * HALF + lax.rem(step, 2) * size
        blocks[...] += cross_blocks(rounded[pl.ds(pl.multiple_of(start, 64), size), :])
        return carry

    lax.fori_loop(0, PARTS * 2, cross_inside, 0)

    load_prior.wait()
    squared = lax.dot_general(
        prior_tile[...],
        prior_tile[...],
        (((0,), (0,)), ((), ())),
        precision=lax.Precision.HIGHEST,
        preferred_element_type=f32,
    )
    mixed, shared, diagonal = pack(
        squared[:LANES, :LANES], squared[:LANES, LANES:], squared[LANES:, LANES:]
    )
    prior_gram[0:LANES, :] = mixed
    prior_gram[LANES:K, :] = shared
    prior_gram[K:, :] = jnp.broadcast_to(diagonal, (8, LANES))

    for copy in halos:
        copy.wait()
    for m in range(PARTS):
        for side in range(2):
            for step in range(2):
                cell = (HALF - 2, 0)[side] + step
                rows = pl.ds(m * HALF * HALF + cell * HALF, HALF)
                value = x_in[side, m, step].astype(f32)
                for h in range(2):
                    coarse[h, rows, :] += value[:, h * LANES : (h + 1) * LANES]
    for side in range(2):
        for other in range(2):
            corner = c_in[side, other].astype(f32)
            for m in range(PARTS):
                for along in range(2):
                    row = (HALF - 2, 0)[other] + along
                    column = (HALF - 2, 0)[side]
                    source = (m * 2 + along) * 2
                    target = pl.ds(m * HALF * HALF + row * HALF + column, 2)
                    value = corner[source : source + 2, :]
                    for h in range(2):
                        coarse[h, target, :] += value[:, h * LANES : (h + 1) * LANES]
    along_x = lax.broadcasted_iota(jnp.int32, (HALF, LANES), 0)
    kept = (along_x >= 2) & (along_x < HALF - 2)
    for m in range(PARTS):
        for side in range(2):
            for step in range(2):
                cell = (HALF - 2, 0)[side] + step
                rows = pl.ds(m * HALF * HALF + cell, HALF, stride=HALF)
                value = y_in[side, m, step].astype(f32)
                place = pl.ds(((m * 2 + side) * 2 + step) * HALF, HALF)
                for h in range(2):
                    total = coarse[h, rows, :] + value[:, h * LANES : (h + 1) * LANES]
                    coarse[h, rows, :] = total
                    border[place, pl.ds(h * LANES, LANES)] = jnp.where(kept, total, 0.0).astype(
                        bf16
                    )
    for m in range(PARTS):
        for side in range(2):
            rows = pl.ds(m * HALF * HALF + (HALF - 2, 0)[side] * HALF, 2 * HALF)
            place = pl.ds((PARTS * 4 + (m * 2 + side) * 2) * HALF, 2 * HALF)
            for h in range(2):
                border[place, pl.ds(h * LANES, LANES)] = coarse[h, rows, :].astype(bf16)

    total = blocks[...]
    half_border = PARTS * 4 * HALF
    for part in range(2):
        total += cross_blocks(border[pl.ds(part * half_border, half_border), :])
    mixed, shared, diagonal = pack(total[0], total[1], total[2])
    packed[0 : LANES // 8, 0:8, :] = mixed.reshape(LANES // 8, 8, LANES)
    packed[LANES // 8 :, 0:8, :] = shared.reshape(LANES // 8, 8, LANES)
    packed[:, 8:9, :] = jnp.broadcast_to(diagonal[None], (MEMBERS, 1, LANES))

    me = gx * 2 + core

    def to_members(source_of, target, send_sem, recv_sem):
        copies = []
        for step in range(1, MEMBERS):
            other = lax.rem(me + step, MEMBERS)
            copies.append(
                pltpu.make_async_remote_copy(
                    src_ref=source_of(other),
                    dst_ref=target.at[me],
                    send_sem=send_sem.at[step],
                    recv_sem=recv_sem.at[step],
                    device_id=(other // 2, 2 * zed + lax.rem(other, 2)),
                    device_id_type=MESH,
                )
            )
        for copy in copies:
            copy.start()
        return copies

    def sum_slots(slots, count):
        total = slots[0]
        for slot in range(1, count):
            total = total + slots[slot]
        return total

    copies = to_members(lambda other: packed.at[other], rs_in, rs_send, rs_recv)
    rs_in[me] = packed[me]

    block = 512

    def finish(step, carry):
        rows = pl.ds(pl.multiple_of(step * block, block), block)
        for h in range(2):
            rounded[rows, pl.ds(h * LANES, LANES)] = coarse[h, rows, :].astype(bf16)
        return carry

    lax.fori_loop(0, PARTS * HALF * HALF // block, finish, 0)
    store = pltpu.make_async_copy(rounded, coarse_ref, store_sem)
    store.start()
    for copy in copies:
        copy.wait()

    z_in[zed] = sum_slots(rs_in, MEMBERS)
    copies = []
    for step in range(1, DEEP):
        copies.append(
            pltpu.make_async_remote_copy(
                src_ref=z_in.at[zed],
                dst_ref=z_in.at[zed],
                send_sem=z_send.at[step],
                recv_sem=z_recv.at[step],
                device_id=(gx, 2 * lax.rem(zed + step, DEEP) + core),
                device_id_type=MESH,
            )
        )
    for copy in copies:
        copy.start()
    for copy in copies:
        copy.wait()

    ag_in[me] = sum_slots(z_in, DEEP)
    for copy in to_members(lambda other: ag_in.at[me], ag_in, ag_send, ag_recv):
        copy.wait()

    count = PARTS * HALF * HALF * RING * RING
    share = 1.0 / count
    sums = ag_in[:, 0:8, :].reshape(K, LANES)
    gram_ref[:K, :] = sums * share + prior_gram[:K, :]
    gram_ref[K:, :] = jnp.broadcast_to(ag_in[0, 8:9, :] * share, (8, LANES)) + prior_gram[K:, :]
    store.wait()


def filter_call(snapshots, prior):
    rows = PARTS * HALF * HALF
    vmem = pltpu.VMEM
    dma = pltpu.SemaphoreType.DMA
    return pl.pallas_call(
        filter_kernel,
        out_shape=(
            jax.ShapeDtypeStruct((rows, K), bf16),
            jax.ShapeDtypeStruct((K + 8, LANES), f32),
        ),
        in_specs=[pl.BlockSpec(memory_space=pltpu.HBM)] * 2,
        out_specs=(pl.BlockSpec(memory_space=pl.ANY), pl.BlockSpec(memory_space=pltpu.VMEM)),
        scratch_shapes=[
            vmem((PARTS, FINE, FINE, K), bf16),
            vmem((K, K), f32),
            vmem((PARTS, FINE, ROWS, K), f32),
            vmem((2, PARTS * SLOTS * 8, LANES), f32),
            vmem((2, rows, LANES), f32),
            vmem((rows, K), bf16),
            vmem((PARTS * 8 * HALF, K), bf16),
            vmem((2, PARTS, 2, HALF, K), bf16),
            vmem((2, PARTS, 2, HALF, K), bf16),
            vmem((2, PARTS, 2, HALF, K), bf16),
            vmem((2, PARTS, 2, HALF, K), bf16),
            vmem((2, 2, 2, 16, LANES), f32),
            vmem((2, 2, 16, K), bf16),
            vmem((2, 2, 16, K), bf16),
            vmem((3, LANES, LANES), f32),
            vmem((MEMBERS, 9, LANES), f32),
            vmem((K + 8, LANES), f32),
            vmem((MEMBERS, 9, LANES), f32),
            vmem((DEEP, 9, LANES), f32),
            vmem((MEMBERS, 9, LANES), f32),
            dma((13,)),
            dma,
            dma((16,)),
            dma((16,)),
            dma((MEMBERS,)),
            dma((MEMBERS,)),
            dma((DEEP,)),
            dma((DEEP,)),
            dma((MEMBERS,)),
            dma((MEMBERS,)),
        ],
        compiler_params=pltpu.CompilerParams(
            collective_id=0, has_side_effects=True, vmem_limit_bytes=48 * 2**20
        ),
        name="filter_and_gram",
    )(snapshots, prior)


def split(value):
    high = value.astype(bf16)
    rest = value - high.astype(f32)
    middle = rest.astype(bf16)
    return high, middle, (rest - middle.astype(f32)).astype(bf16)


def factor_panels(work, upper, inverse):
    below = lax.broadcasted_iota(jnp.int32, (PANEL, 128), 0)
    for first in range(0, K, PANEL):
        rows = pl.ds(first, PANEL)
        strip = work[rows, :]
        columns = [
            jnp.broadcast_to(strip[:, first + k : first + k + 1], (PANEL, 128))
            for k in range(PANEL)
        ]
        tiles = [strip[:, t : t + 128] for t in range(0, 2 * K, 128)]
        pivots = jnp.zeros((PANEL, 128), f32)
        for j in range(PANEL):
            pivot = jnp.broadcast_to(columns[j][j : j + 1, :], (PANEL, 128))
            pivots = jnp.where(below == j, pivot, pivots)
            if j == PANEL - 1:
                break
            factor = jnp.where(below > j, columns[j] / pivot, 0.0)
            for k in range(j + 1, PANEL):
                columns[k] -= factor * jnp.broadcast_to(columns[k][j : j + 1, :], (PANEL, 128))
            tiles = [t - factor * jnp.broadcast_to(t[j : j + 1, :], (PANEL, 128)) for t in tiles]
        scale = lax.rsqrt(pivots)
        strip = jnp.concatenate([t * scale for t in tiles], axis=1)
        upper[rows, :] = strip[:, :K]
        inverse[rows, :] = strip[:, K:]
        done = first + PANEL
        if done < K:
            high, middle, low = split(strip)
            left = jnp.concatenate([high, high, middle, high, low, middle], axis=0)
            right = jnp.concatenate([high, middle, high, low, high, middle], axis=0)
            work[done:, :] -= lax.dot_general(
                left[:, done:K], right, (((0,), (0,)), ((), ())), preferred_element_type=f32
            )


def factor_kernel(
    coarse_ref, gram_ref, modes_ref, upper_ref, rows_in, work, upper, inverse, out, load_sem, store_sem
):
    load = pltpu.make_async_copy(coarse_ref, rows_in, load_sem)
    load.start()
    row = lax.broadcasted_iota(jnp.int32, (K, K), 0)
    column = lax.broadcasted_iota(jnp.int32, (K, K), 1)
    shared = gram_ref[LANES:K, :]
    turned = shared.T
    upper_half = row[:LANES, :LANES] <= column[:LANES, :LANES]
    equal = row[:LANES, :LANES] == column[:LANES, :LANES]
    work[:LANES, :LANES] = jnp.where(upper_half, shared, turned)
    work[:LANES, LANES:K] = gram_ref[:LANES, :]
    work[LANES:, :LANES] = jnp.zeros((LANES, LANES), f32)
    work[LANES:, LANES:K] = jnp.where(
        equal, gram_ref[K : K + 1, :], jnp.where(upper_half, turned, shared)
    )
    work[:, K:] = jnp.where(row == column, 1.0, 0.0)
    factor_panels(work, upper, inverse)
    upper_ref[...] = jnp.where(row <= column, upper[...], 0.0)
    high, middle, low = split(inverse[...].T)
    load.wait()
    count = rows_in.shape[0]
    block = 512
    stores = []
    for step in range(count // block):
        rows = pl.ds(step * block, block)
        part = rows_in[rows, :]
        value = jnp.dot(part, high, preferred_element_type=f32)
        value += jnp.dot(part, middle, preferred_element_type=f32)
        out[rows, :] = value
        stores.append(
            pltpu.make_async_copy(out.at[rows], modes_ref.at[rows], store_sem.at[step])
        )
        stores[-1].start()
    for store in stores:
        store.wait()


def factor_call(coarse, gram):
    rows = coarse.shape[0]
    vmem = pltpu.VMEM
    return pl.pallas_call(
        factor_kernel,
        out_shape=(jax.ShapeDtypeStruct((rows, K), f32), jax.ShapeDtypeStruct((K, K), f32)),
        in_specs=[pl.BlockSpec(memory_space=pl.ANY), pl.BlockSpec(memory_space=pltpu.VMEM)],
        out_specs=(pl.BlockSpec(memory_space=pl.ANY), pl.BlockSpec(memory_space=pltpu.VMEM)),
        scratch_shapes=[
            vmem((rows, K), bf16),
            vmem((K, 2 * K), f32),
            vmem((K, K), f32),
            vmem((K, K), f32),
            vmem((rows, K), f32),
            pltpu.SemaphoreType.DMA,
            pltpu.SemaphoreType.DMA((rows // 512,)),
        ],
        compiler_params=pltpu.CompilerParams(vmem_limit_bytes=48 * 2**20),
        name="factor_and_modes",
    )(coarse, gram)


def shards(snapshots, prior):
    coarse, gram = filter_call(snapshots, prior)
    modes, upper = factor_call(coarse, gram)
    return (modes.reshape(PARTS, HALF, HALF, K), upper)


def solution(mesh):
    return jax.shard_map(
        shards,
        mesh=mesh,
        in_specs=(P(None, "gx", "gy", None), P()),
        out_specs=(P(None, "gx", "gy", None), P()),
        check_vma=False,
    )
```

```python
import functools

import jax
import jax.numpy as jnp
from jax import lax
from jax.experimental import pallas as pl
from jax.experimental.pallas import tpu as pltpu
from jax.sharding import PartitionSpec as P

f32 = jnp.float32
bf16 = jnp.bfloat16
MESH = pl.DeviceIdType.MESH
TAPS = (1, 8, 28, 56, 70, 56, 28, 8, 1)
RING = 16
PARTS = 3
FINE = 64
HALF = 32
K = 256
LANES = 128
ROWS = 40
GROUP = 4
SLOTS = 40
SIDE = 4
DEEP = 8
MEMBERS = 32
PANEL = 32


def y_matrix():
    shape = (GROUP * ROWS, GROUP * FINE)
    row = lax.broadcasted_iota(jnp.int32, shape, 0)
    column = lax.broadcasted_iota(jnp.int32, shape, 1)
    slab = row // ROWS
    index = row % ROWS
    cell = jnp.where(index < HALF, index, jnp.where(index < HALF + 2, index - HALF - 2, index - 2))
    offset = column % FINE - 2 * cell + 4
    offset = jnp.where((slab == column // FINE) & (index < HALF + 4), offset, -1)
    taps = jnp.zeros(shape, f32)
    for place, tap in enumerate(TAPS):
        taps = jnp.where(offset == place, tap / 65536.0, taps)
    return jnp.where(slab % 2 == 1, 8.0 * taps, taps).astype(bf16)


def x_sum(load, cell):
    total = None

    def pair(first, second, low, high):
        have = [load(2 * q + second) for q in (low, high) if 0 <= q < HALF]
        if not have:
            return None
        value = have[0] if len(have) == 1 else have[0] + have[1]
        return value if first == 1.0 else first * value

    terms = [
        pair(1.0, 0, cell - 2, cell + 2),
        pair(28.0, 0, cell - 1, cell + 1),
        pair(70.0, 0, cell, -1),
        pair(1.0, 1, cell - 2, cell + 1),
        pair(7.0, 1, cell - 1, cell),
    ]
    for term in terms:
        if term is not None:
            total = term if total is None else total + term
    return total


def x_cell(slot):
    return slot if slot < HALF else (slot - HALF - 2 if slot < HALF + 2 else slot - 2)


def cross(left, right):
    contract = (((0,), (0,)), ((), ()))
    return lax.dot_general(left, right, contract, preferred_element_type=f32)


def cross_blocks(part):
    top = cross(part[:, :LANES], part)
    return jnp.stack([top[:, :LANES], top[:, LANES:], cross(part[:, LANES:], part[:, LANES:])])


def pack(low, mixed, high):
    row = lax.broadcasted_iota(jnp.int32, (LANES, LANES), 0)
    column = lax.broadcasted_iota(jnp.int32, (LANES, LANES), 1)
    shared = jnp.where(row <= column, low, high)
    diagonal = jnp.sum(jnp.where(row == column, high, 0.0), axis=0, keepdims=True)
    return mixed, shared, diagonal


def arrivals(ref, sem):
    pltpu.make_async_copy(ref, ref, sem).wait()


def filter_kernel(
    snap_ref,
    coarse_ref,
    gram_ref,
    tile,
    ysum,
    edge,
    coarse,
    rounded,
    border,
    x_out,
    x_in,
    y_out,
    y_in,
    c_stage,
    c_out,
    c_in,
    blocks,
    packed,
    rs_in,
    z_in,
    ag_in,
    load_sem,
    store_sem,
    halo_send,
    halo_recv,
    sum_send,
    sum_recv,
):
    gx = lax.axis_index("gx")
    gy = lax.axis_index("gy")
    core = lax.rem(gy, 2)
    zed = gy // 2
    gx_next, gx_last = lax.rem(gx + 1, RING), lax.rem(gx + RING - 1, RING)
    gy_next, gy_last = lax.rem(gy + 1, RING), lax.rem(gy + RING - 1, RING)

    slabs = 32
    loads = []
    for m in range(PARTS):
        for q in range(FINE // slabs):
            place = (m, pl.ds(q * slabs, slabs))
            loads.append(
                pltpu.make_async_copy(
                    snap_ref.at[place], tile.at[place], load_sem.at[len(loads)]
                )
            )
    for load in loads:
        load.start()

    barrier = pltpu.get_barrier_semaphore()

    def greet(peer):
        pl.semaphore_signal(barrier, inc=1, device_id=peer, device_id_type=MESH)

    def greet_z(step, carry):
        greet((gx, 2 * lax.rem(zed + step, DEEP) + core))
        return carry

    def greet_member(step, carry):
        other = lax.rem(gx * 2 + core + step, MEMBERS)
        greet((other // 2, 2 * zed + lax.rem(other, 2)))
        return carry

    lax.fori_loop(1, DEEP, greet_z, 0)
    lax.fori_loop(1, MEMBERS, greet_member, 0)
    for oy in (gy_last, gy_next):
        for ox in (gx_last, gx, gx_next):
            greet((ox, oy))
    for ox in (gx_last, gx_next):
        greet((ox, gy))

    def send(source, target, peer, kind):
        pltpu.make_async_remote_copy(
            src_ref=source,
            dst_ref=target,
            send_sem=halo_send.at[kind],
            recv_sem=halo_recv.at[kind],
            device_id=peer,
            device_id_type=MESH,
        ).start()

    c_stage[:, :, :, 8:, :] = jnp.zeros((2, 2, 2, 8, LANES), f32)
    taps = y_matrix()
    for m in range(PARTS):
        for q in range(FINE // slabs):
            loads[m * (FINE // slabs) + q].wait()
            for g in range(slabs // GROUP):
                first = q * slabs + g * GROUP
                fine = tile[m, pl.ds(first, GROUP)].reshape(GROUP * FINE, K)
                sums = jnp.dot(taps, fine, preferred_element_type=f32)
                ysum[m, pl.ds(first, GROUP)] = sums.reshape(GROUP, ROWS, K)

        for side in range(2):
            for step in range(2):
                cell = (-2, HALF)[side] + step
                value = x_sum(lambda x: ysum[m, x, pl.ds(0, HALF), :], cell)
                x_out[side, m, step] = value.astype(bf16)

        for slot in range(HALF + 4):
            value = x_sum(lambda x: ysum[m, x, pl.ds(HALF, 8), :], x_cell(slot))
            rows = pl.ds(m * (SLOTS * 8) + slot * 8, 8)
            edge[0, rows, :] = value[:, :LANES]
            edge[1, rows, :] = value[:, LANES:]
        for side in range(2):
            for step in range(2):
                start = m * SLOTS * 8 + side * 2 + step
                picked = [edge[h, pl.ds(start, HALF, stride=8), :] for h in range(2)]
                y_out[side, m, step] = jnp.concatenate(picked, axis=1).astype(bf16)
            for other in range(2):
                for along in range(2):
                    start = m * SLOTS * 8 + (HALF + other * 2 + along) * 8 + side * 2
                    for h in range(2):
                        c_stage[h, side, other, pl.ds((m * 2 + along) * 2, 2), :] = edge[
                            h, pl.ds(start, 2), :
                        ]

        if m >= 1:
            if m == 1:
                pl.semaphore_wait(barrier, DEEP - 1 + MEMBERS - 1 + 8)
            for part in (0, 1) if m == 1 else (m,):
                send(x_out.at[0, part], x_in.at[0, part], (gx_last, gy), 0)
                send(x_out.at[1, part], x_in.at[1, part], (gx_next, gy), 0)
                send(y_out.at[0, part], y_in.at[0, part], (gx, gy_last), 1)
                send(y_out.at[1, part], y_in.at[1, part], (gx, gy_next), 1)

    for side, oy in ((0, gy_last), (1, gy_next)):
        for other, ox in ((0, gx_last), (1, gx_next)):
            corner = [c_stage[h, side, other] for h in range(2)]
            c_out[side, other] = jnp.concatenate(corner, axis=1).astype(bf16)
            send(c_out.at[side, other], c_in.at[side, other], (ox, oy), 2)

    along_y = lax.broadcasted_iota(jnp.int32, (16, LANES), 0)

    def inside(step, carry):
        m = step // 2
        row = pl.multiple_of(lax.rem(step, 2) * 16, 16)
        y = along_y + row
        kept = (y >= 2) & (y < HALF - 2)
        for h in range(2):
            lanes = pl.ds(h * LANES, LANES)
            for cell in range(HALF):
                value = x_sum(lambda x: ysum[m, x, pl.ds(row, 16), lanes], cell)
                rows = pl.ds(pl.multiple_of(m * (HALF * HALF) + cell * HALF + row, 16), 16)
                coarse[h, rows, :] = value
                rounded[rows, lanes] = jnp.where(kept, value, 0.0).astype(bf16)
        return carry

    lax.fori_loop(0, PARTS * 2, inside, 0)

    blocks[...] = jnp.zeros(blocks.shape, f32)
    size = (HALF - 4) * HALF // 2

    def cross_inside(step, carry):
        start = (step // 2) * HALF * HALF + 2 * HALF + lax.rem(step, 2) * size
        blocks[...] += cross_blocks(rounded[pl.ds(pl.multiple_of(start, 64), size), :])
        return carry

    lax.fori_loop(0, PARTS * 2, cross_inside, 0)

    for kind, arrived in enumerate((x_in, y_in, c_in)):
        arrivals(arrived, halo_recv.at[kind])
    for m in range(PARTS):
        for side in range(2):
            for step in range(2):
                cell = (HALF - 2, 0)[side] + step
                rows = pl.ds(m * HALF * HALF + cell * HALF, HALF)
                value = x_in[side, m, step].astype(f32)
                for h in range(2):
                    coarse[h, rows, :] += value[:, h * LANES : (h + 1) * LANES]
    for side in range(2):
        for other in range(2):
            corner = c_in[side, other].astype(f32)
            for m in range(PARTS):
                for along in range(2):
                    row = (HALF - 2, 0)[other] + along
                    column = (HALF - 2, 0)[side]
                    source = (m * 2 + along) * 2
                    target = pl.ds(m * HALF * HALF + row * HALF + column, 2)
                    value = corner[source : source + 2, :]
                    for h in range(2):
                        coarse[h, target, :] += value[:, h * LANES : (h + 1) * LANES]
    along_x = lax.broadcasted_iota(jnp.int32, (HALF, LANES), 0)
    kept = (along_x >= 2) & (along_x < HALF - 2)
    for m in range(PARTS):
        for side in range(2):
            for step in range(2):
                cell = (HALF - 2, 0)[side] + step
                rows = pl.ds(m * HALF * HALF + cell, HALF, stride=HALF)
                value = y_in[side, m, step].astype(f32)
                place = pl.ds(((m * 2 + side) * 2 + step) * HALF, HALF)
                for h in range(2):
                    total = coarse[h, rows, :] + value[:, h * LANES : (h + 1) * LANES]
                    coarse[h, rows, :] = total
                    border[place, pl.ds(h * LANES, LANES)] = jnp.where(kept, total, 0.0).astype(
                        bf16
                    )
    for m in range(PARTS):
        for side in range(2):
            rows = pl.ds(m * HALF * HALF + (HALF - 2, 0)[side] * HALF, 2 * HALF)
            place = pl.ds((PARTS * 4 + (m * 2 + side) * 2) * HALF, 2 * HALF)
            for h in range(2):
                border[place, pl.ds(h * LANES, LANES)] = coarse[h, rows, :].astype(bf16)

    total = blocks[...]
    half_border = PARTS * 4 * HALF
    for part in range(2):
        total += cross_blocks(border[pl.ds(part * half_border, half_border), :])
    mixed, shared, diagonal = pack(total[0], total[1], total[2])
    packed[0 : LANES // 8, 0:8, :] = mixed.reshape(LANES // 8, 8, LANES)
    packed[LANES // 8 :, 0:8, :] = shared.reshape(LANES // 8, 8, LANES)
    packed[:, 8:9, :] = jnp.broadcast_to(diagonal[None], (MEMBERS, 1, LANES))

    me = gx * 2 + core

    at_x, at_y = gx // SIDE, lax.rem(gx, SIDE)

    def to_members(source_of, target, phase):
        for far in range(SIDE, -1, -1):
            for dx in range(SIDE):
                for dy in range(SIDE):
                    if min(dx, SIDE - dx) + min(dy, SIDE - dy) != far:
                        continue
                    peer = SIDE * lax.rem(at_x + dx, SIDE) + lax.rem(at_y + dy, SIDE)
                    for dc in range(2):
                        if dx + dy + dc == 0:
                            continue
                        there = lax.rem(core + dc, 2)
                        pltpu.make_async_remote_copy(
                            src_ref=source_of(peer * 2 + there),
                            dst_ref=target.at[me],
                            send_sem=sum_send.at[phase],
                            recv_sem=sum_recv.at[phase],
                            device_id=(peer, 2 * zed + there),
                            device_id_type=MESH,
                        ).start()

    def sum_slots(slots, count):
        total = slots[0]
        for slot in range(1, count):
            total = total + slots[slot]
        return total

    to_members(lambda other: packed.at[other], rs_in, 0)
    rs_in[me] = packed[me]

    block = 512

    def finish(step, carry):
        rows = pl.ds(pl.multiple_of(step * block, block), block)
        for h in range(2):
            rounded[rows, pl.ds(h * LANES, LANES)] = coarse[h, rows, :].astype(bf16)
        return carry

    lax.fori_loop(0, PARTS * HALF * HALF // block, finish, 0)
    store = pltpu.make_async_copy(rounded, coarse_ref, store_sem)
    store.start()
    arrivals(rs_in.at[pl.ds(0, MEMBERS - 1)], sum_recv.at[0])

    z_in[zed] = sum_slots(rs_in, MEMBERS)
    for step in (4, 3, 5, 2, 6, 1, 7):
        pltpu.make_async_remote_copy(
            src_ref=z_in.at[zed],
            dst_ref=z_in.at[zed],
            send_sem=sum_send.at[1],
            recv_sem=sum_recv.at[1],
            device_id=(gx, 2 * lax.rem(zed + step, DEEP) + core),
            device_id_type=MESH,
        ).start()
    arrivals(z_in.at[pl.ds(0, DEEP - 1)], sum_recv.at[1])

    ag_in[me] = sum_slots(z_in, DEEP)
    to_members(lambda other: ag_in.at[me], ag_in, 2)
    arrivals(ag_in.at[pl.ds(0, MEMBERS - 1)], sum_recv.at[2])

    count = PARTS * HALF * HALF * RING * RING
    share = 1.0 / count
    gram_ref[:K, :] = ag_in[:, 0:8, :].reshape(K, LANES) * share
    gram_ref[K:, :] = jnp.broadcast_to(ag_in[0, 8:9, :] * share, (8, LANES))
    for kind, sent in enumerate((x_out, y_out, c_out)):
        arrivals(sent, halo_send.at[kind])
    arrivals(packed.at[pl.ds(0, MEMBERS - 1)], sum_send.at[0])
    arrivals(z_in.at[pl.ds(0, DEEP - 1)], sum_send.at[1])
    arrivals(ag_in.at[pl.ds(0, MEMBERS - 1)], sum_send.at[2])
    store.wait()


def filter_call(snapshots):
    rows = PARTS * HALF * HALF
    vmem = pltpu.VMEM
    dma = pltpu.SemaphoreType.DMA
    return pl.pallas_call(
        filter_kernel,
        out_shape=(
            jax.ShapeDtypeStruct((rows, K), bf16),
            jax.ShapeDtypeStruct((K + 8, LANES), f32),
        ),
        in_specs=[pl.BlockSpec(memory_space=pltpu.HBM)],
        out_specs=(pl.BlockSpec(memory_space=pl.ANY), pl.BlockSpec(memory_space=pltpu.VMEM)),
        scratch_shapes=[
            vmem((PARTS, FINE, FINE, K), bf16),
            vmem((PARTS, FINE, ROWS, K), f32),
            vmem((2, PARTS * SLOTS * 8, LANES), f32),
            vmem((2, rows, LANES), f32),
            vmem((rows, K), bf16),
            vmem((PARTS * 8 * HALF, K), bf16),
            vmem((2, PARTS, 2, HALF, K), bf16),
            vmem((2, PARTS, 2, HALF, K), bf16),
            vmem((2, PARTS, 2, HALF, K), bf16),
            vmem((2, PARTS, 2, HALF, K), bf16),
            vmem((2, 2, 2, 16, LANES), f32),
            vmem((2, 2, 16, K), bf16),
            vmem((2, 2, 16, K), bf16),
            vmem((3, LANES, LANES), f32),
            vmem((MEMBERS, 9, LANES), f32),
            vmem((MEMBERS, 9, LANES), f32),
            vmem((DEEP, 9, LANES), f32),
            vmem((MEMBERS, 9, LANES), f32),
            dma((PARTS * 2,)),
            dma,
            dma((3,)),
            dma((3,)),
            dma((3,)),
            dma((3,)),
        ],
        compiler_params=pltpu.CompilerParams(
            collective_id=0, has_side_effects=True, vmem_limit_bytes=48 * 2**20
        ),
        name="filter_and_gram",
    )(snapshots)


def split(value):
    high = value.astype(bf16)
    rest = value - high.astype(f32)
    middle = rest.astype(bf16)
    return high, middle, (rest - middle.astype(f32)).astype(bf16)


def factor_panels(work, upper, inverse):
    place = lax.broadcasted_iota(jnp.int32, (8, LANES), 0)
    parts = PANEL // 8
    contract = (((0,), (0,)), ((), ()))

    def spread(value, row):
        return jnp.broadcast_to(value[row : row + 1, :], (8, LANES))

    later = None
    for first in range(0, K, PANEL):
        rows = pl.ds(first, PANEL)
        low = 0 if first < LANES else LANES
        high = low + 3 * LANES
        strip = work[rows, low:high]
        columns = [
            [
                jnp.broadcast_to(
                    strip[8 * t : 8 * t + 8, first - low + k : first - low + k + 1], (8, LANES)
                )
                if t >= k // 8
                else None
                for t in range(parts)
            ]
            for k in range(PANEL)
        ]
        tiles = [
            [strip[8 * t : 8 * t + 8, q * LANES : (q + 1) * LANES] for q in range(3)]
            for t in range(parts)
        ]
        pivots = [None] * parts
        pivot = spread(columns[0][0], 0)
        for j in range(PANEL):
            top, row = divmod(j, 8)
            column = columns[j]
            pivots[top] = pivot if row == 0 else jnp.where(place == row, pivot, pivots[top])
            if j == PANEL - 1:
                break
            if j == 2 and later is not None:
                later()
                later = None
            over = 1.0 / pivot
            beside = spread(column[(j + 1) // 8], (j + 1) % 8)
            pivot = spread(columns[j + 1][(j + 1) // 8], (j + 1) % 8) - (beside * beside) * over
            factor = {}
            for t in range(top if row < 7 else top + 1, parts):
                value = column[t] * over
                factor[t] = jnp.where(place > row, value, 0.0) if t == top else value
            for k in range(j + 1, PANEL):
                across = spread(column[k // 8], k % 8)
                for t in range(k // 8, parts):
                    columns[k][t] = columns[k][t] - factor[t] * across
            source = [spread(value, row) for value in tiles[top]]
            for t in factor:
                tiles[t] = [tiles[t][q] - factor[t] * source[q] for q in range(3)]
        strip = jnp.concatenate(
            [
                jnp.concatenate([value * lax.rsqrt(pivots[t]) for value in tiles[t]], axis=1)
                for t in range(parts)
            ],
            axis=0,
        )
        if low == 0:
            upper[rows, :] = strip[:, :K]
            inverse[rows, :LANES] = strip[:, K:]
            inverse[rows, LANES:] = jnp.zeros((PANEL, LANES), f32)
        else:
            upper[rows, :LANES] = jnp.zeros((PANEL, LANES), f32)
            upper[rows, LANES:] = strip[:, :LANES]
            inverse[rows, :] = strip[:, LANES:]
        done = first + PANEL
        if done < K:
            great, middle, small = split(strip)
            left = jnp.concatenate([great, great, middle, great, small, middle], axis=0)
            right = jnp.concatenate([great, middle, great, small, great, middle], axis=0)

            def update(start, stop, left=left, right=right, low=low, high=high):
                work[start:stop, low:high] -= lax.dot_general(
                    left[:, start - low : stop - low], right, contract, preferred_element_type=f32
                )

            update(done, done + PANEL)
            if done + PANEL < K:
                later = functools.partial(update, done + PANEL, K)


def factor_kernel(
    coarse_ref, gram_ref, prior_ref, modes_ref, upper_ref, rows_in, work, upper, inverse, out, load_sem, store_sem
):
    load = pltpu.make_async_copy(coarse_ref, rows_in, load_sem)
    load.start()
    row = lax.broadcasted_iota(jnp.int32, (K, K), 0)
    column = lax.broadcasted_iota(jnp.int32, (K, K), 1)
    prior_gram = lax.dot_general(
        prior_ref[...],
        prior_ref[...],
        (((0,), (0,)), ((), ())),
        precision=lax.Precision.HIGHEST,
        preferred_element_type=f32,
    )
    shared = gram_ref[LANES:K, :]
    turned = shared.T
    upper_half = row[:LANES, :LANES] <= column[:LANES, :LANES]
    equal = row[:LANES, :LANES] == column[:LANES, :LANES]
    work[:LANES, :LANES] = jnp.where(upper_half, shared, turned) + prior_gram[:LANES, :LANES]
    work[:LANES, LANES:K] = gram_ref[:LANES, :] + prior_gram[:LANES, LANES:]
    work[LANES:, :LANES] = jnp.zeros((LANES, LANES), f32)
    work[LANES:, LANES:K] = (
        jnp.where(equal, gram_ref[K : K + 1, :], jnp.where(upper_half, turned, shared))
        + prior_gram[LANES:, LANES:]
    )
    work[:, K:] = jnp.where(row == column, 1.0, 0.0)
    factor_panels(work, upper, inverse)
    upper_ref[...] = jnp.where(row <= column, upper[...], 0.0)
    high, middle, low = split(inverse[...].T)
    load.wait()
    count = rows_in.shape[0]
    block = 512
    for step in range(count // block):
        rows = pl.ds(step * block, block)
        part = rows_in[rows, :]
        value = jnp.dot(part, high, preferred_element_type=f32)
        value += jnp.dot(part, middle, preferred_element_type=f32)
        out[rows, :] = value
        pltpu.make_async_copy(out.at[rows], modes_ref.at[rows], store_sem).start()
    pltpu.make_async_copy(out, modes_ref, store_sem).wait()


def factor_call(coarse, gram, prior):
    rows = coarse.shape[0]
    vmem = pltpu.VMEM
    return pl.pallas_call(
        factor_kernel,
        out_shape=(jax.ShapeDtypeStruct((rows, K), f32), jax.ShapeDtypeStruct((K, K), f32)),
        in_specs=[pl.BlockSpec(memory_space=pl.ANY)] + [pl.BlockSpec(memory_space=pltpu.VMEM)] * 2,
        out_specs=(pl.BlockSpec(memory_space=pl.ANY), pl.BlockSpec(memory_space=pltpu.VMEM)),
        scratch_shapes=[
            vmem((rows, K), bf16),
            vmem((K, 2 * K), f32),
            vmem((K, K), f32),
            vmem((K, K), f32),
            vmem((rows, K), f32),
            pltpu.SemaphoreType.DMA,
            pltpu.SemaphoreType.DMA,
        ],
        compiler_params=pltpu.CompilerParams(vmem_limit_bytes=48 * 2**20),
        name="factor_and_modes",
    )(coarse, gram, prior)


def shards(snapshots, prior):
    coarse, gram = filter_call(snapshots)
    modes, upper = factor_call(coarse, gram, prior)
    return (modes.reshape(PARTS, HALF, HALF, K), upper)


def solution(mesh):
    return jax.shard_map(
        shards,
        mesh=mesh,
        in_specs=(P(None, "gx", "gy", None), P()),
        out_specs=(P(None, "gx", "gy", None), P()),
        check_vma=False,
    )
```

```python
import functools

import jax
import jax.numpy as jnp
from jax import lax
from jax.experimental import pallas as pl
from jax.experimental.pallas import tpu as pltpu
from jax.sharding import PartitionSpec as P

f32 = jnp.float32
bf16 = jnp.bfloat16
MESH = pl.DeviceIdType.MESH
TAPS = (1, 8, 28, 56, 70, 56, 28, 8, 1)
RING = 16
PARTS = 3
FINE = 64
HALF = 32
K = 256
LANES = 128
STRIP = 16
GROUP = 4
SLOTS = 40
SIDE = 4
DEEP = 8
MEMBERS = 32
PANEL = 32


def tap_matrix(row_slab, cell, column_slab, y, used):
    offset = jnp.where((row_slab == column_slab) & used, y - 2 * cell + 4, -1)
    taps = jnp.zeros(offset.shape, f32)
    for place, tap in enumerate(TAPS):
        taps = jnp.where(offset == place, tap / 65536.0, taps)
    return jnp.where(row_slab % 2 == 1, 8.0 * taps, taps).astype(bf16)


def inside_taps():
    shape = (GROUP * HALF, GROUP * FINE)
    row = lax.broadcasted_iota(jnp.int32, shape, 0)
    column = lax.broadcasted_iota(jnp.int32, shape, 1)
    return tap_matrix(row // HALF, row % HALF, column // FINE, column % FINE, row >= 0)


def outside_taps():
    shape = (8 * 8, 8 * 2 * STRIP)
    row = lax.broadcasted_iota(jnp.int32, shape, 0)
    column = lax.broadcasted_iota(jnp.int32, shape, 1)
    index = row % 8
    cell = jnp.where(index < 2, index - 2, index + HALF - 2)
    along = column % (2 * STRIP)
    y = jnp.where(along < STRIP, along, along + FINE - 2 * STRIP)
    return tap_matrix(row // 8, cell, column // (2 * STRIP), y, index < 4)


def x_sum(load, cell):
    total = None

    def pair(first, second, low, high):
        have = [load(2 * q + second) for q in (low, high) if 0 <= q < HALF]
        if not have:
            return None
        value = have[0] if len(have) == 1 else have[0] + have[1]
        return value if first == 1.0 else first * value

    terms = [
        pair(1.0, 0, cell - 2, cell + 2),
        pair(28.0, 0, cell - 1, cell + 1),
        pair(70.0, 0, cell, -1),
        pair(1.0, 1, cell - 2, cell + 1),
        pair(7.0, 1, cell - 1, cell),
    ]
    for term in terms:
        if term is not None:
            total = term if total is None else total + term
    return total


def x_cell(slot):
    return slot if slot < HALF else (slot - HALF - 2 if slot < HALF + 2 else slot - 2)


def cross(left, right):
    contract = (((0,), (0,)), ((), ()))
    return lax.dot_general(left, right, contract, preferred_element_type=f32)


def cross_blocks(part):
    top = cross(part[:, :LANES], part)
    return jnp.stack([top[:, :LANES], top[:, LANES:], cross(part[:, LANES:], part[:, LANES:])])


def pack(low, mixed, high):
    row = lax.broadcasted_iota(jnp.int32, (LANES, LANES), 0)
    column = lax.broadcasted_iota(jnp.int32, (LANES, LANES), 1)
    shared = jnp.where(row <= column, low, high)
    diagonal = jnp.sum(jnp.where(row == column, high, 0.0), axis=0, keepdims=True)
    return mixed, shared, diagonal


def arrivals(ref, sem):
    pltpu.make_async_copy(ref, ref, sem).wait()


def filter_kernel(
    snap_ref,
    coarse_ref,
    gram_ref,
    tile,
    strip,
    ysum,
    yside,
    edge,
    coarse,
    rounded,
    border,
    x_out,
    x_in,
    y_out,
    y_in,
    c_stage,
    c_out,
    c_in,
    blocks,
    packed,
    rs_in,
    z_in,
    ag_in,
    load_sem,
    store_sem,
    halo_send,
    halo_recv,
    sum_send,
    sum_recv,
):
    gx = lax.axis_index("gx")
    gy = lax.axis_index("gy")
    core = lax.rem(gy, 2)
    zed = gy // 2
    gx_next, gx_last = lax.rem(gx + 1, RING), lax.rem(gx + RING - 1, RING)
    gy_next, gy_last = lax.rem(gy + 1, RING), lax.rem(gy + RING - 1, RING)

    for first in (0, FINE - GROUP):
        place = (slice(None), pl.ds(first, GROUP))
        pltpu.make_async_copy(snap_ref.at[place], tile.at[place], load_sem.at[0]).start()
    for side in range(2):
        pltpu.make_async_copy(
            snap_ref.at[:, :, pl.ds(side * (FINE - STRIP), STRIP)],
            strip.at[:, :, pl.ds(side * STRIP, STRIP)],
            load_sem.at[1],
        ).start()
    slabs = (FINE - 2 * GROUP) // 2
    loads = []
    for m in range(PARTS):
        for q in range(2):
            place = (m, pl.ds(GROUP + q * slabs, slabs))
            loads.append(
                pltpu.make_async_copy(
                    snap_ref.at[place], tile.at[place], load_sem.at[2 + len(loads)]
                )
            )
    for load in loads:
        load.start()

    barrier = pltpu.get_barrier_semaphore()

    def greet(peer):
        pl.semaphore_signal(barrier, inc=1, device_id=peer, device_id_type=MESH)

    def greet_z(step, carry):
        greet((gx, 2 * lax.rem(zed + step, DEEP) + core))
        return carry

    def greet_member(step, carry):
        other = lax.rem(gx * 2 + core + step, MEMBERS)
        greet((other // 2, 2 * zed + lax.rem(other, 2)))
        return carry

    lax.fori_loop(1, DEEP, greet_z, 0)
    lax.fori_loop(1, MEMBERS, greet_member, 0)
    for oy in (gy_last, gy_next):
        for ox in (gx_last, gx, gx_next):
            greet((ox, oy))
    for ox in (gx_last, gx_next):
        greet((ox, gy))

    def send(source, target, peer, kind):
        pltpu.make_async_remote_copy(
            src_ref=source,
            dst_ref=target,
            send_sem=halo_send.at[kind],
            recv_sem=halo_recv.at[kind],
            device_id=peer,
            device_id_type=MESH,
        ).start()

    c_stage[:, :, :, 8:, :] = jnp.zeros((2, 2, 2, 8, LANES), f32)
    taps = inside_taps()

    def y_pass(m, first):
        fine = tile[m, pl.ds(first, GROUP)].reshape(GROUP * FINE, K)
        sums = jnp.dot(taps, fine, preferred_element_type=f32)
        ysum[m, pl.ds(first, GROUP)] = sums.reshape(GROUP, HALF, K)

    arrivals(tile.at[:, pl.ds(0, 2 * GROUP)], load_sem.at[0])
    for m in range(PARTS):
        y_pass(m, 0)
        y_pass(m, FINE - GROUP)
        for side in range(2):
            for step in range(2):
                cell = (-2, HALF)[side] + step
                value = x_sum(lambda x: ysum[m, x], cell)
                x_out[side, m, step] = value.astype(bf16)

    outer = outside_taps()
    arrivals(strip, load_sem.at[1])
    for m in range(PARTS):
        for g in range(FINE // 8):
            fine = strip[m, pl.ds(g * 8, 8)].reshape(8 * 2 * STRIP, K)
            sums = jnp.dot(outer, fine, preferred_element_type=f32)
            yside[m, pl.ds(g * 8, 8)] = sums.reshape(8, 8, K)
        for slot in range(HALF + 4):
            value = x_sum(lambda x: yside[m, x], x_cell(slot))
            rows = pl.ds(m * (SLOTS * 8) + slot * 8, 8)
            edge[0, rows, :] = value[:, :LANES]
            edge[1, rows, :] = value[:, LANES:]
        for side in range(2):
            for step in range(2):
                start = m * SLOTS * 8 + side * 2 + step
                picked = [edge[h, pl.ds(start, HALF, stride=8), :] for h in range(2)]
                y_out[side, m, step] = jnp.concatenate(picked, axis=1).astype(bf16)
            for other in range(2):
                for along in range(2):
                    start = m * SLOTS * 8 + (HALF + other * 2 + along) * 8 + side * 2
                    for h in range(2):
                        c_stage[h, side, other, pl.ds((m * 2 + along) * 2, 2), :] = edge[
                            h, pl.ds(start, 2), :
                        ]

    pl.semaphore_wait(barrier, DEEP - 1 + MEMBERS - 1 + 8)
    send(x_out.at[0], x_in.at[0], (gx_last, gy), 0)
    send(x_out.at[1], x_in.at[1], (gx_next, gy), 0)
    send(y_out.at[0], y_in.at[0], (gx, gy_last), 1)
    send(y_out.at[1], y_in.at[1], (gx, gy_next), 1)
    for side, oy in ((0, gy_last), (1, gy_next)):
        for other, ox in ((0, gx_last), (1, gx_next)):
            corner = [c_stage[h, side, other] for h in range(2)]
            c_out[side, other] = jnp.concatenate(corner, axis=1).astype(bf16)
            send(c_out.at[side, other], c_in.at[side, other], (ox, oy), 2)

    along_y = lax.broadcasted_iota(jnp.int32, (16, LANES), 0)
    blocks[...] = jnp.zeros(blocks.shape, f32)
    for m in range(PARTS):
        for q in range(2):
            loads[m * 2 + q].wait()
            for g in range(slabs // GROUP):
                y_pass(m, GROUP + q * slabs + g * GROUP)

        def inside(step, carry, m=m):
            row = pl.multiple_of(step * 16, 16)
            y = along_y + row
            kept = (y >= 2) & (y < HALF - 2)
            for h in range(2):
                lanes = pl.ds(h * LANES, LANES)
                for cell in range(HALF):
                    value = x_sum(lambda x: ysum[m, x, pl.ds(row, 16), lanes], cell)
                    rows = pl.ds(pl.multiple_of(m * (HALF * HALF) + cell * HALF + row, 16), 16)
                    coarse[h, rows, :] = value
                    rounded[rows, lanes] = jnp.where(kept, value, 0.0).astype(bf16)
            return carry

        lax.fori_loop(0, 2, inside, 0)
        rows = pl.ds(m * HALF * HALF + 2 * HALF, (HALF - 4) * HALF)
        blocks[...] += cross_blocks(rounded[rows, :])

    for kind, arrived in enumerate((x_in, y_in, c_in)):
        arrivals(arrived, halo_recv.at[kind])
    for m in range(PARTS):
        for side in range(2):
            for step in range(2):
                cell = (HALF - 2, 0)[side] + step
                rows = pl.ds(m * HALF * HALF + cell * HALF, HALF)
                value = x_in[side, m, step].astype(f32)
                for h in range(2):
                    coarse[h, rows, :] += value[:, h * LANES : (h + 1) * LANES]
    for side in range(2):
        for other in range(2):
            corner = c_in[side, other].astype(f32)
            for m in range(PARTS):
                for along in range(2):
                    row = (HALF - 2, 0)[other] + along
                    column = (HALF - 2, 0)[side]
                    source = (m * 2 + along) * 2
                    target = pl.ds(m * HALF * HALF + row * HALF + column, 2)
                    value = corner[source : source + 2, :]
                    for h in range(2):
                        coarse[h, target, :] += value[:, h * LANES : (h + 1) * LANES]
    along_x = lax.broadcasted_iota(jnp.int32, (HALF, LANES), 0)
    kept = (along_x >= 2) & (along_x < HALF - 2)
    for m in range(PARTS):
        for side in range(2):
            for step in range(2):
                cell = (HALF - 2, 0)[side] + step
                rows = pl.ds(m * HALF * HALF + cell, HALF, stride=HALF)
                value = y_in[side, m, step].astype(f32)
                place = pl.ds(((m * 2 + side) * 2 + step) * HALF, HALF)
                for h in range(2):
                    total = coarse[h, rows, :] + value[:, h * LANES : (h + 1) * LANES]
                    coarse[h, rows, :] = total
                    border[place, pl.ds(h * LANES, LANES)] = jnp.where(kept, total, 0.0).astype(
                        bf16
                    )
    for m in range(PARTS):
        for side in range(2):
            rows = pl.ds(m * HALF * HALF + (HALF - 2, 0)[side] * HALF, 2 * HALF)
            place = pl.ds((PARTS * 4 + (m * 2 + side) * 2) * HALF, 2 * HALF)
            for h in range(2):
                border[place, pl.ds(h * LANES, LANES)] = coarse[h, rows, :].astype(bf16)

    total = blocks[...]
    half_border = PARTS * 4 * HALF
    for part in range(2):
        total += cross_blocks(border[pl.ds(part * half_border, half_border), :])
    mixed, shared, diagonal = pack(total[0], total[1], total[2])
    packed[0 : LANES // 8, 0:8, :] = mixed.reshape(LANES // 8, 8, LANES)
    packed[LANES // 8 :, 0:8, :] = shared.reshape(LANES // 8, 8, LANES)
    packed[:, 8:9, :] = jnp.broadcast_to(diagonal[None], (MEMBERS, 1, LANES))

    me = gx * 2 + core

    at_x, at_y = gx // SIDE, lax.rem(gx, SIDE)

    def to_members(source_of, target, phase):
        for far in range(SIDE, -1, -1):
            for dx in range(SIDE):
                for dy in range(SIDE):
                    if min(dx, SIDE - dx) + min(dy, SIDE - dy) != far:
                        continue
                    peer = SIDE * lax.rem(at_x + dx, SIDE) + lax.rem(at_y + dy, SIDE)
                    for dc in range(2):
                        if dx + dy + dc == 0:
                            continue
                        there = lax.rem(core + dc, 2)
                        pltpu.make_async_remote_copy(
                            src_ref=source_of(peer * 2 + there),
                            dst_ref=target.at[me],
                            send_sem=sum_send.at[phase],
                            recv_sem=sum_recv.at[phase],
                            device_id=(peer, 2 * zed + there),
                            device_id_type=MESH,
                        ).start()

    def sum_slots(slots, count):
        total = slots[0]
        for slot in range(1, count):
            total = total + slots[slot]
        return total

    to_members(lambda other: packed.at[other], rs_in, 0)
    rs_in[me] = packed[me]

    block = 512

    def finish(step, carry):
        rows = pl.ds(pl.multiple_of(step * block, block), block)
        for h in range(2):
            rounded[rows, pl.ds(h * LANES, LANES)] = coarse[h, rows, :].astype(bf16)
        return carry

    lax.fori_loop(0, PARTS * HALF * HALF // block, finish, 0)
    store = pltpu.make_async_copy(rounded, coarse_ref, store_sem)
    store.start()
    arrivals(rs_in.at[pl.ds(0, MEMBERS - 1)], sum_recv.at[0])

    z_in[zed] = sum_slots(rs_in, MEMBERS)
    for step in (4, 3, 5, 2, 6, 1, 7):
        pltpu.make_async_remote_copy(
            src_ref=z_in.at[zed],
            dst_ref=z_in.at[zed],
            send_sem=sum_send.at[1],
            recv_sem=sum_recv.at[1],
            device_id=(gx, 2 * lax.rem(zed + step, DEEP) + core),
            device_id_type=MESH,
        ).start()
    arrivals(z_in.at[pl.ds(0, DEEP - 1)], sum_recv.at[1])

    ag_in[me] = sum_slots(z_in, DEEP)
    to_members(lambda other: ag_in.at[me], ag_in, 2)
    arrivals(ag_in.at[pl.ds(0, MEMBERS - 1)], sum_recv.at[2])

    count = PARTS * HALF * HALF * RING * RING
    share = 1.0 / count
    gram_ref[:K, :] = ag_in[:, 0:8, :].reshape(K, LANES) * share
    gram_ref[K:, :] = jnp.broadcast_to(ag_in[0, 8:9, :] * share, (8, LANES))
    for kind, sent in enumerate((x_out, y_out, c_out)):
        arrivals(sent, halo_send.at[kind])
    arrivals(packed.at[pl.ds(0, MEMBERS - 1)], sum_send.at[0])
    arrivals(z_in.at[pl.ds(0, DEEP - 1)], sum_send.at[1])
    arrivals(ag_in.at[pl.ds(0, MEMBERS - 1)], sum_send.at[2])
    store.wait()


def filter_call(snapshots):
    rows = PARTS * HALF * HALF
    vmem = pltpu.VMEM
    dma = pltpu.SemaphoreType.DMA
    return pl.pallas_call(
        filter_kernel,
        out_shape=(
            jax.ShapeDtypeStruct((rows, K), bf16),
            jax.ShapeDtypeStruct((K + 8, LANES), f32),
        ),
        in_specs=[pl.BlockSpec(memory_space=pltpu.HBM)],
        out_specs=(pl.BlockSpec(memory_space=pl.ANY), pl.BlockSpec(memory_space=pltpu.VMEM)),
        scratch_shapes=[
            vmem((PARTS, FINE, FINE, K), bf16),
            vmem((PARTS, FINE, 2 * STRIP, K), bf16),
            vmem((PARTS, FINE, HALF, K), f32),
            vmem((PARTS, FINE, 8, K), f32),
            vmem((2, PARTS * SLOTS * 8, LANES), f32),
            vmem((2, rows, LANES), f32),
            vmem((rows, K), bf16),
            vmem((PARTS * 8 * HALF, K), bf16),
            vmem((2, PARTS, 2, HALF, K), bf16),
            vmem((2, PARTS, 2, HALF, K), bf16),
            vmem((2, PARTS, 2, HALF, K), bf16),
            vmem((2, PARTS, 2, HALF, K), bf16),
            vmem((2, 2, 2, 16, LANES), f32),
            vmem((2, 2, 16, K), bf16),
            vmem((2, 2, 16, K), bf16),
            vmem((3, LANES, LANES), f32),
            vmem((MEMBERS, 9, LANES), f32),
            vmem((MEMBERS, 9, LANES), f32),
            vmem((DEEP, 9, LANES), f32),
            vmem((MEMBERS, 9, LANES), f32),
            dma((2 + PARTS * 2,)),
            dma,
            dma((3,)),
            dma((3,)),
            dma((3,)),
            dma((3,)),
        ],
        compiler_params=pltpu.CompilerParams(
            collective_id=0, has_side_effects=True, vmem_limit_bytes=48 * 2**20
        ),
        name="filter_and_gram",
    )(snapshots)


def split(value):
    high = value.astype(bf16)
    rest = value - high.astype(f32)
    middle = rest.astype(bf16)
    return high, middle, (rest - middle.astype(f32)).astype(bf16)


def factor_panels(work, upper, inverse, beside):
    place = lax.broadcasted_iota(jnp.int32, (8, LANES), 0)
    parts = PANEL // 8
    contract = (((0,), (0,)), ((), ()))

    def spread(value, row):
        return jnp.broadcast_to(value[row : row + 1, :], (8, LANES))

    later = None
    for first in range(0, K, PANEL):
        rows = pl.ds(first, PANEL)
        low = 0 if first < LANES else LANES
        high = low + 3 * LANES
        strip = work[rows, low:high]
        columns = [
            [
                jnp.broadcast_to(
                    strip[8 * t : 8 * t + 8, first - low + k : first - low + k + 1], (8, LANES)
                )
                if t >= k // 8
                else None
                for t in range(parts)
            ]
            for k in range(PANEL)
        ]
        tiles = [
            [strip[8 * t : 8 * t + 8, q * LANES : (q + 1) * LANES] for q in range(3)]
            for t in range(parts)
        ]
        pivots = [None] * parts
        pivot = spread(columns[0][0], 0)
        for j in range(PANEL):
            top, row = divmod(j, 8)
            column = columns[j]
            pivots[top] = pivot if row == 0 else jnp.where(place == row, pivot, pivots[top])
            if j == PANEL - 1:
                break
            if j == 2 and later is not None:
                later()
                later = None
            if j == 6 and first >= LANES:
                beside((first - LANES) // PANEL)
            over = 1.0 / pivot
            nearby = spread(column[(j + 1) // 8], (j + 1) % 8)
            pivot = spread(columns[j + 1][(j + 1) // 8], (j + 1) % 8) - (nearby * nearby) * over
            factor = {}
            for t in range(top if row < 7 else top + 1, parts):
                value = column[t] * over
                factor[t] = jnp.where(place > row, value, 0.0) if t == top else value
            for k in range(j + 1, PANEL):
                across = spread(column[k // 8], k % 8)
                for t in range(k // 8, parts):
                    columns[k][t] = columns[k][t] - factor[t] * across
            source = [spread(value, row) for value in tiles[top]]
            for t in factor:
                tiles[t] = [tiles[t][q] - factor[t] * source[q] for q in range(3)]
        strip = jnp.concatenate(
            [
                jnp.concatenate([value * lax.rsqrt(pivots[t]) for value in tiles[t]], axis=1)
                for t in range(parts)
            ],
            axis=0,
        )
        if low == 0:
            upper[rows, :] = strip[:, :K]
            inverse[rows, :LANES] = strip[:, K:]
            inverse[rows, LANES:] = jnp.zeros((PANEL, LANES), f32)
        else:
            upper[rows, :LANES] = jnp.zeros((PANEL, LANES), f32)
            upper[rows, LANES:] = strip[:, :LANES]
            inverse[rows, :] = strip[:, LANES:]
        done = first + PANEL
        if done < K:
            great, middle, small = split(strip)
            left = jnp.concatenate([great, great, middle, great, small, middle], axis=0)
            right = jnp.concatenate([great, middle, great, small, great, middle], axis=0)

            def update(start, stop, left=left, right=right, low=low, high=high):
                work[start:stop, low:high] -= lax.dot_general(
                    left[:, start - low : stop - low], right, contract, preferred_element_type=f32
                )

            update(done, done + PANEL)
            if done + PANEL < K:
                later = functools.partial(update, done + PANEL, K)


def factor_kernel(
    coarse_ref, gram_ref, prior_ref, modes_ref, upper_ref, rows_in, work, upper, inverse, out, load_sem, store_sem
):
    load = pltpu.make_async_copy(coarse_ref, rows_in, load_sem)
    load.start()
    row = lax.broadcasted_iota(jnp.int32, (K, K), 0)
    column = lax.broadcasted_iota(jnp.int32, (K, K), 1)

    def exact(left, right):
        return lax.dot_general(
            left,
            right,
            (((0,), (0,)), ((), ())),
            precision=lax.Precision.HIGHEST,
            preferred_element_type=f32,
        )

    prior_top = exact(prior_ref[:LANES, :LANES], prior_ref[:LANES, :])
    prior_low = exact(prior_ref[:, LANES:], prior_ref[:, LANES:])
    shared = gram_ref[LANES:K, :]
    turned = shared.T
    upper_half = row[:LANES, :LANES] <= column[:LANES, :LANES]
    equal = row[:LANES, :LANES] == column[:LANES, :LANES]
    work[:LANES, :LANES] = jnp.where(upper_half, shared, turned) + prior_top[:, :LANES]
    work[:LANES, LANES:K] = gram_ref[:LANES, :] + prior_top[:, LANES:]
    work[LANES:, :LANES] = jnp.zeros((LANES, LANES), f32)
    work[LANES:, LANES:K] = (
        jnp.where(equal, gram_ref[K : K + 1, :], jnp.where(upper_half, turned, shared))
        + prior_low
    )
    work[:, K:] = jnp.where(row == column, 1.0, 0.0)
    count = rows_in.shape[0]
    block = count // 4

    def give(half, rows):
        return pltpu.make_async_copy(
            out.at[half, rows], modes_ref.at[rows, pl.ds(half * LANES, LANES)], store_sem.at[half]
        )

    def halves(value):
        great, middle, _ = split(value)
        return jnp.concatenate([great, middle], axis=0)

    quarter = []

    def first_lanes(q):
        if q == 0:
            load.wait()
            quarter.append(halves(inverse[:LANES, :LANES].T))
        rows = pl.ds(q * block, block)
        part = rows_in[rows, :LANES]
        part = jnp.concatenate([part, part], axis=1)
        out[0, rows, :] = jnp.dot(part, quarter[0], preferred_element_type=f32)
        give(0, rows).start()

    factor_panels(work, upper, inverse, first_lanes)
    rest = halves(inverse[LANES:, :].T)
    for q in range(4):
        rows = pl.ds(q * block, block)
        part = rows_in[rows, :]
        part = jnp.concatenate([part, part], axis=1)
        out[1, rows, :] = jnp.dot(part, rest, preferred_element_type=f32)
        give(1, rows).start()
        if q == 0:
            upper[...] = jnp.where(row <= column, upper[...], 0.0)
            store_upper = pltpu.make_async_copy(upper, upper_ref, store_sem.at[2])
            store_upper.start()
    store_upper.wait()
    for half in range(2):
        give(half, pl.ds(0, count)).wait()


def factor_call(coarse, gram, prior):
    rows = coarse.shape[0]
    vmem = pltpu.VMEM
    return pl.pallas_call(
        factor_kernel,
        out_shape=(jax.ShapeDtypeStruct((rows, K), f32), jax.ShapeDtypeStruct((K, K), f32)),
        in_specs=[pl.BlockSpec(memory_space=pl.ANY)] + [pl.BlockSpec(memory_space=pltpu.VMEM)] * 2,
        out_specs=(pl.BlockSpec(memory_space=pl.ANY), pl.BlockSpec(memory_space=pl.ANY)),
        scratch_shapes=[
            vmem((rows, K), bf16),
            vmem((K, 2 * K), f32),
            vmem((K, K), f32),
            vmem((K, K), f32),
            vmem((2, rows, LANES), f32),
            pltpu.SemaphoreType.DMA,
            pltpu.SemaphoreType.DMA((3,)),
        ],
        compiler_params=pltpu.CompilerParams(vmem_limit_bytes=48 * 2**20),
        name="factor_and_modes",
    )(coarse, gram, prior)


def shards(snapshots, prior):
    coarse, gram = filter_call(snapshots)
    modes, upper = factor_call(coarse, gram, prior)
    return (modes.reshape(PARTS, HALF, HALF, K), upper)


def solution(mesh):
    return jax.shard_map(
        shards,
        mesh=mesh,
        in_specs=(P(None, "gx", "gy", None), P()),
        out_specs=(P(None, "gx", "gy", None), P()),
        check_vma=False,
    )
```

```python
import functools

import jax
import jax.numpy as jnp
from jax import lax
from jax.experimental import pallas as pl
from jax.experimental.pallas import tpu as pltpu
from jax.sharding import PartitionSpec as P

f32 = jnp.float32
bf16 = jnp.bfloat16
MESH = pl.DeviceIdType.MESH
TAPS = (1, 8, 28, 56, 70, 56, 28, 8, 1)
RING = 16
PARTS = 3
FINE = 64
HALF = 32
K = 256
LANES = 128
STRIP = 16
GROUP = 4
SLOTS = 40
SIDE = 4
DEEP = 8
MEMBERS = 32
PANEL = 32


def tap_matrix(row_slab, cell, column_slab, y, used):
    offset = jnp.where((row_slab == column_slab) & used, y - 2 * cell + 4, -1)
    taps = jnp.zeros(offset.shape, f32)
    for place, tap in enumerate(TAPS):
        taps = jnp.where(offset == place, tap / 65536.0, taps)
    return jnp.where(row_slab % 2 == 1, 8.0 * taps, taps).astype(bf16)


def inside_taps():
    shape = (GROUP * HALF, GROUP * FINE)
    row = lax.broadcasted_iota(jnp.int32, shape, 0)
    column = lax.broadcasted_iota(jnp.int32, shape, 1)
    return tap_matrix(row // HALF, row % HALF, column // FINE, column % FINE, row >= 0)


def outside_taps():
    shape = (8 * 8, 8 * 2 * STRIP)
    row = lax.broadcasted_iota(jnp.int32, shape, 0)
    column = lax.broadcasted_iota(jnp.int32, shape, 1)
    index = row % 8
    cell = jnp.where(index < 2, index - 2, index + HALF - 2)
    along = column % (2 * STRIP)
    y = jnp.where(along < STRIP, along, along + FINE - 2 * STRIP)
    return tap_matrix(row // 8, cell, column // (2 * STRIP), y, index < 4)


def x_sum(load, cell):
    total = None

    def pair(first, second, low, high):
        have = [load(2 * q + second) for q in (low, high) if 0 <= q < HALF]
        if not have:
            return None
        value = have[0] if len(have) == 1 else have[0] + have[1]
        return value if first == 1.0 else first * value

    terms = [
        pair(1.0, 0, cell - 2, cell + 2),
        pair(28.0, 0, cell - 1, cell + 1),
        pair(70.0, 0, cell, -1),
        pair(1.0, 1, cell - 2, cell + 1),
        pair(7.0, 1, cell - 1, cell),
    ]
    for term in terms:
        if term is not None:
            total = term if total is None else total + term
    return total


def x_cell(slot):
    return slot if slot < HALF else (slot - HALF - 2 if slot < HALF + 2 else slot - 2)


def cross(left, right):
    contract = (((0,), (0,)), ((), ()))
    return lax.dot_general(left, right, contract, preferred_element_type=f32)


def cross_blocks(part):
    top = cross(part[:, :LANES], part)
    return jnp.stack([top[:, :LANES], top[:, LANES:], cross(part[:, LANES:], part[:, LANES:])])


def pack(low, mixed, high):
    row = lax.broadcasted_iota(jnp.int32, (LANES, LANES), 0)
    column = lax.broadcasted_iota(jnp.int32, (LANES, LANES), 1)
    shared = jnp.where(row <= column, low, high)
    diagonal = jnp.sum(jnp.where(row == column, high, 0.0), axis=0, keepdims=True)
    return mixed, shared, diagonal


def arrivals(ref, sem):
    pltpu.make_async_copy(ref, ref, sem).wait()


def filter_kernel(
    snap_ref,
    coarse_ref,
    gram_ref,
    tile,
    strip,
    ysum,
    yside,
    edge,
    coarse,
    rounded,
    border,
    x_out,
    x_in,
    y_out,
    y_in,
    c_stage,
    c_out,
    c_in,
    blocks,
    packed,
    rs_in,
    z_in,
    ag_in,
    load_sem,
    store_sem,
    halo_send,
    halo_recv,
    sum_send,
    sum_recv,
):
    gx = lax.axis_index("gx")
    gy = lax.axis_index("gy")
    core = lax.rem(gy, 2)
    zed = gy // 2
    gx_next, gx_last = lax.rem(gx + 1, RING), lax.rem(gx + RING - 1, RING)
    gy_next, gy_last = lax.rem(gy + 1, RING), lax.rem(gy + RING - 1, RING)

    for first in (0, FINE - GROUP):
        place = (slice(None), pl.ds(first, GROUP))
        pltpu.make_async_copy(snap_ref.at[place], tile.at[place], load_sem.at[0]).start()
    for m in range(PARTS):
        for side in range(2):
            pltpu.make_async_copy(
                snap_ref.at[m, :, pl.ds(side * (FINE - STRIP), STRIP)],
                strip.at[m, :, pl.ds(side * STRIP, STRIP)],
                load_sem.at[1 + m],
            ).start()
    slabs = (FINE - 2 * GROUP) // 2
    loads = []
    for m in range(PARTS):
        for q in range(2):
            place = (m, pl.ds(GROUP + q * slabs, slabs))
            loads.append(
                pltpu.make_async_copy(
                    snap_ref.at[place], tile.at[place], load_sem.at[1 + PARTS + len(loads)]
                )
            )

    barrier = pltpu.get_barrier_semaphore()

    def greet(peer):
        pl.semaphore_signal(barrier, inc=1, device_id=peer, device_id_type=MESH)

    def greet_z(step, carry):
        greet((gx, 2 * lax.rem(zed + step, DEEP) + core))
        return carry

    def greet_member(step, carry):
        other = lax.rem(gx * 2 + core + step, MEMBERS)
        greet((other // 2, 2 * zed + lax.rem(other, 2)))
        return carry

    lax.fori_loop(1, DEEP, greet_z, 0)
    lax.fori_loop(1, MEMBERS, greet_member, 0)
    for oy in (gy_last, gy_next):
        for ox in (gx_last, gx, gx_next):
            greet((ox, oy))
    for ox in (gx_last, gx_next):
        greet((ox, gy))

    def send(source, target, peer, kind):
        pltpu.make_async_remote_copy(
            src_ref=source,
            dst_ref=target,
            send_sem=halo_send.at[kind],
            recv_sem=halo_recv.at[kind],
            device_id=peer,
            device_id_type=MESH,
        ).start()

    c_stage[:, :, :, 8:, :] = jnp.zeros((2, 2, 2, 8, LANES), f32)
    taps = inside_taps()

    def y_pass(m, first):
        fine = tile[m, pl.ds(first, GROUP)].reshape(GROUP * FINE, K)
        sums = jnp.dot(taps, fine, preferred_element_type=f32)
        ysum[m, pl.ds(first, GROUP)] = sums.reshape(GROUP, HALF, K)

    arrivals(tile.at[:, pl.ds(0, 2 * GROUP)], load_sem.at[0])
    loads[0].start()
    loads[1].start()
    for m in range(PARTS):
        y_pass(m, 0)
        y_pass(m, FINE - GROUP)
        for side in range(2):
            for step in range(2):
                cell = (-2, HALF)[side] + step
                value = x_sum(lambda x: ysum[m, x], cell)
                x_out[side, m, step] = value.astype(bf16)

    outer = outside_taps()
    for m in range(PARTS):
        arrivals(strip.at[m], load_sem.at[1 + m])
        if m + 1 < PARTS:
            loads[2 * m + 2].start()
            loads[2 * m + 3].start()
        for g in range(FINE // 8):
            fine = strip[m, pl.ds(g * 8, 8)].reshape(8 * 2 * STRIP, K)
            sums = jnp.dot(outer, fine, preferred_element_type=f32)
            yside[m, pl.ds(g * 8, 8)] = sums.reshape(8, 8, K)
        for slot in range(HALF + 4):
            value = x_sum(lambda x: yside[m, x], x_cell(slot))
            rows = pl.ds(m * (SLOTS * 8) + slot * 8, 8)
            edge[0, rows, :] = value[:, :LANES]
            edge[1, rows, :] = value[:, LANES:]
        for side in range(2):
            for step in range(2):
                start = m * SLOTS * 8 + side * 2 + step
                picked = [edge[h, pl.ds(start, HALF, stride=8), :] for h in range(2)]
                y_out[side, m, step] = jnp.concatenate(picked, axis=1).astype(bf16)
            for other in range(2):
                for along in range(2):
                    start = m * SLOTS * 8 + (HALF + other * 2 + along) * 8 + side * 2
                    for h in range(2):
                        c_stage[h, side, other, pl.ds((m * 2 + along) * 2, 2), :] = edge[
                            h, pl.ds(start, 2), :
                        ]

    pl.semaphore_wait(barrier, DEEP - 1 + MEMBERS - 1 + 8)
    send(x_out.at[0], x_in.at[0], (gx_last, gy), 0)
    send(x_out.at[1], x_in.at[1], (gx_next, gy), 0)
    send(y_out.at[0], y_in.at[0], (gx, gy_last), 1)
    send(y_out.at[1], y_in.at[1], (gx, gy_next), 1)
    for side, oy in ((0, gy_last), (1, gy_next)):
        for other, ox in ((0, gx_last), (1, gx_next)):
            corner = [c_stage[h, side, other] for h in range(2)]
            c_out[side, other] = jnp.concatenate(corner, axis=1).astype(bf16)
            send(c_out.at[side, other], c_in.at[side, other], (ox, oy), 2)

    along_y = lax.broadcasted_iota(jnp.int32, (16, LANES), 0)
    blocks[...] = jnp.zeros(blocks.shape, f32)
    for m in range(PARTS):
        for q in range(2):
            loads[m * 2 + q].wait()
            for g in range(slabs // GROUP):
                y_pass(m, GROUP + q * slabs + g * GROUP)

        def inside(step, carry, m=m):
            row = pl.multiple_of(step * 16, 16)
            y = along_y + row
            kept = (y >= 2) & (y < HALF - 2)
            for h in range(2):
                lanes = pl.ds(h * LANES, LANES)
                for cell in range(HALF):
                    value = x_sum(lambda x: ysum[m, x, pl.ds(row, 16), lanes], cell)
                    rows = pl.ds(pl.multiple_of(m * (HALF * HALF) + cell * HALF + row, 16), 16)
                    coarse[h, rows, :] = value
                    rounded[rows, lanes] = jnp.where(kept, value, 0.0).astype(bf16)
            return carry

        lax.fori_loop(0, 2, inside, 0)
        rows = pl.ds(m * HALF * HALF + 2 * HALF, (HALF - 4) * HALF)
        blocks[...] += cross_blocks(rounded[rows, :])

    for kind, arrived in enumerate((x_in, y_in, c_in)):
        arrivals(arrived, halo_recv.at[kind])
    for m in range(PARTS):
        for side in range(2):
            for step in range(2):
                cell = (HALF - 2, 0)[side] + step
                rows = pl.ds(m * HALF * HALF + cell * HALF, HALF)
                value = x_in[side, m, step].astype(f32)
                for h in range(2):
                    coarse[h, rows, :] += value[:, h * LANES : (h + 1) * LANES]
    for side in range(2):
        for other in range(2):
            corner = c_in[side, other].astype(f32)
            for m in range(PARTS):
                for along in range(2):
                    row = (HALF - 2, 0)[other] + along
                    column = (HALF - 2, 0)[side]
                    source = (m * 2 + along) * 2
                    target = pl.ds(m * HALF * HALF + row * HALF + column, 2)
                    value = corner[source : source + 2, :]
                    for h in range(2):
                        coarse[h, target, :] += value[:, h * LANES : (h + 1) * LANES]
    along_x = lax.broadcasted_iota(jnp.int32, (HALF, LANES), 0)
    kept = (along_x >= 2) & (along_x < HALF - 2)
    for m in range(PARTS):
        for side in range(2):
            for step in range(2):
                cell = (HALF - 2, 0)[side] + step
                rows = pl.ds(m * HALF * HALF + cell, HALF, stride=HALF)
                value = y_in[side, m, step].astype(f32)
                place = pl.ds(((m * 2 + side) * 2 + step) * HALF, HALF)
                for h in range(2):
                    total = coarse[h, rows, :] + value[:, h * LANES : (h + 1) * LANES]
                    coarse[h, rows, :] = total
                    border[place, pl.ds(h * LANES, LANES)] = jnp.where(kept, total, 0.0).astype(
                        bf16
                    )
    for m in range(PARTS):
        for side in range(2):
            rows = pl.ds(m * HALF * HALF + (HALF - 2, 0)[side] * HALF, 2 * HALF)
            place = pl.ds((PARTS * 4 + (m * 2 + side) * 2) * HALF, 2 * HALF)
            for h in range(2):
                border[place, pl.ds(h * LANES, LANES)] = coarse[h, rows, :].astype(bf16)

    total = blocks[...]
    total += cross_blocks(border[...])
    mixed, shared, diagonal = pack(total[0], total[1], total[2])
    packed[0 : LANES // 8, 0:8, :] = mixed.reshape(LANES // 8, 8, LANES)
    packed[LANES // 8 :, 0:8, :] = shared.reshape(LANES // 8, 8, LANES)
    packed[:, 8:9, :] = jnp.broadcast_to(diagonal[None], (MEMBERS, 1, LANES))

    me = gx * 2 + core

    at_x, at_y = gx // SIDE, lax.rem(gx, SIDE)

    def to_members(source_of, target, phase):
        for far in range(SIDE, -1, -1):
            for dx in range(SIDE):
                for dy in range(SIDE):
                    if min(dx, SIDE - dx) + min(dy, SIDE - dy) != far:
                        continue
                    peer = SIDE * lax.rem(at_x + dx, SIDE) + lax.rem(at_y + dy, SIDE)
                    for dc in range(2):
                        if dx + dy + dc == 0:
                            continue
                        there = lax.rem(core + dc, 2)
                        pltpu.make_async_remote_copy(
                            src_ref=source_of(peer * 2 + there),
                            dst_ref=target.at[me],
                            send_sem=sum_send.at[phase],
                            recv_sem=sum_recv.at[phase],
                            device_id=(peer, 2 * zed + there),
                            device_id_type=MESH,
                        ).start()

    def sum_slots(slots, count):
        total = slots[0]
        for slot in range(1, count):
            total = total + slots[slot]
        return total

    to_members(lambda other: packed.at[other], rs_in, 0)
    rs_in[me] = packed[me]

    block = 512

    def finish(step, carry):
        rows = pl.ds(pl.multiple_of(step * block, block), block)
        for h in range(2):
            rounded[rows, pl.ds(h * LANES, LANES)] = coarse[h, rows, :].astype(bf16)
        return carry

    lax.fori_loop(0, PARTS * HALF * HALF // block, finish, 0)
    store = pltpu.make_async_copy(rounded, coarse_ref, store_sem)
    store.start()
    arrivals(rs_in.at[pl.ds(0, MEMBERS - 1)], sum_recv.at[0])

    z_in[zed] = sum_slots(rs_in, MEMBERS)
    for step in (4, 3, 5, 2, 6, 1, 7):
        pltpu.make_async_remote_copy(
            src_ref=z_in.at[zed],
            dst_ref=z_in.at[zed],
            send_sem=sum_send.at[1],
            recv_sem=sum_recv.at[1],
            device_id=(gx, 2 * lax.rem(zed + step, DEEP) + core),
            device_id_type=MESH,
        ).start()
    arrivals(z_in.at[pl.ds(0, DEEP - 1)], sum_recv.at[1])

    ag_in[me] = sum_slots(z_in, DEEP)
    to_members(lambda other: ag_in.at[me], ag_in, 2)
    arrivals(ag_in.at[pl.ds(0, MEMBERS - 1)], sum_recv.at[2])

    count = PARTS * HALF * HALF * RING * RING
    share = 1.0 / count
    gram_ref[:K, :] = ag_in[:, 0:8, :].reshape(K, LANES) * share
    gram_ref[K:, :] = jnp.broadcast_to(ag_in[0, 8:9, :] * share, (8, LANES))
    for kind, sent in enumerate((x_out, y_out, c_out)):
        arrivals(sent, halo_send.at[kind])
    arrivals(packed.at[pl.ds(0, MEMBERS - 1)], sum_send.at[0])
    arrivals(z_in.at[pl.ds(0, DEEP - 1)], sum_send.at[1])
    arrivals(ag_in.at[pl.ds(0, MEMBERS - 1)], sum_send.at[2])
    store.wait()


def filter_call(snapshots):
    rows = PARTS * HALF * HALF
    vmem = pltpu.VMEM
    dma = pltpu.SemaphoreType.DMA
    return pl.pallas_call(
        filter_kernel,
        out_shape=(
            jax.ShapeDtypeStruct((rows, K), bf16),
            jax.ShapeDtypeStruct((K + 8, LANES), f32),
        ),
        in_specs=[pl.BlockSpec(memory_space=pltpu.HBM)],
        out_specs=(pl.BlockSpec(memory_space=pl.ANY), pl.BlockSpec(memory_space=pltpu.VMEM)),
        scratch_shapes=[
            vmem((PARTS, FINE, FINE, K), bf16),
            vmem((PARTS, FINE, 2 * STRIP, K), bf16),
            vmem((PARTS, FINE, HALF, K), f32),
            vmem((PARTS, FINE, 8, K), f32),
            vmem((2, PARTS * SLOTS * 8, LANES), f32),
            vmem((2, rows, LANES), f32),
            vmem((rows, K), bf16),
            vmem((PARTS * 8 * HALF, K), bf16),
            vmem((2, PARTS, 2, HALF, K), bf16),
            vmem((2, PARTS, 2, HALF, K), bf16),
            vmem((2, PARTS, 2, HALF, K), bf16),
            vmem((2, PARTS, 2, HALF, K), bf16),
            vmem((2, 2, 2, 16, LANES), f32),
            vmem((2, 2, 16, K), bf16),
            vmem((2, 2, 16, K), bf16),
            vmem((3, LANES, LANES), f32),
            vmem((MEMBERS, 9, LANES), f32),
            vmem((MEMBERS, 9, LANES), f32),
            vmem((DEEP, 9, LANES), f32),
            vmem((MEMBERS, 9, LANES), f32),
            dma((1 + PARTS * 3,)),
            dma,
            dma((3,)),
            dma((3,)),
            dma((3,)),
            dma((3,)),
        ],
        compiler_params=pltpu.CompilerParams(
            collective_id=0, has_side_effects=True, vmem_limit_bytes=48 * 2**20
        ),
        name="filter_and_gram",
    )(snapshots)


def split(value):
    high = value.astype(bf16)
    rest = value - high.astype(f32)
    middle = rest.astype(bf16)
    return high, middle, (rest - middle.astype(f32)).astype(bf16)


def factor_panels(work, upper, inverse, beside):
    place = lax.broadcasted_iota(jnp.int32, (8, LANES), 0)
    parts = PANEL // 8
    contract = (((0,), (0,)), ((), ()))

    def spread(value, row):
        return jnp.broadcast_to(value[row : row + 1, :], (8, LANES))

    later = None
    for first in range(0, K, PANEL):
        rows = pl.ds(first, PANEL)
        low = 0 if first < LANES else LANES
        high = low + 3 * LANES
        strip = work[rows, low:high]
        columns = [
            [
                jnp.broadcast_to(
                    strip[8 * t : 8 * t + 8, first - low + k : first - low + k + 1], (8, LANES)
                )
                if t >= k // 8
                else None
                for t in range(parts)
            ]
            for k in range(PANEL)
        ]
        tiles = [
            [strip[8 * t : 8 * t + 8, q * LANES : (q + 1) * LANES] for q in range(3)]
            for t in range(parts)
        ]
        pivots = [None] * parts
        pivot = spread(columns[0][0], 0)
        for j in range(PANEL):
            top, row = divmod(j, 8)
            column = columns[j]
            pivots[top] = pivot if row == 0 else jnp.where(place == row, pivot, pivots[top])
            if j == PANEL - 1:
                break
            if j == 2 and later is not None:
                later()
                later = None
            if j == 6 and first >= LANES:
                beside((first - LANES) // PANEL)
            over = 1.0 / pivot
            nearby = spread(column[(j + 1) // 8], (j + 1) % 8)
            pivot = spread(columns[j + 1][(j + 1) // 8], (j + 1) % 8) - (nearby * nearby) * over
            factor = {}
            for t in range(top if row < 7 else top + 1, parts):
                value = column[t] * over
                factor[t] = jnp.where(place > row, value, 0.0) if t == top else value
            for k in range(j + 1, PANEL):
                across = spread(column[k // 8], k % 8)
                for t in range(k // 8, parts):
                    columns[k][t] = columns[k][t] - factor[t] * across
            source = [spread(value, row) for value in tiles[top]]
            for t in factor:
                tiles[t] = [tiles[t][q] - factor[t] * source[q] for q in range(3)]
        strip = jnp.concatenate(
            [
                jnp.concatenate([value * lax.rsqrt(pivots[t]) for value in tiles[t]], axis=1)
                for t in range(parts)
            ],
            axis=0,
        )
        if low == 0:
            upper[rows, :] = strip[:, :K]
            inverse[rows, :LANES] = strip[:, K:]
            inverse[rows, LANES:] = jnp.zeros((PANEL, LANES), f32)
        else:
            upper[rows, :LANES] = jnp.zeros((PANEL, LANES), f32)
            upper[rows, LANES:] = strip[:, :LANES]
            inverse[rows, :] = strip[:, LANES:]
        done = first + PANEL
        if done < K:
            great, middle, small = split(strip)
            left = jnp.concatenate([great, great, middle, great, small, middle], axis=0)
            right = jnp.concatenate([great, middle, great, small, great, middle], axis=0)

            def update(start, stop, left=left, right=right, low=low, high=high):
                work[start:stop, low:high] -= lax.dot_general(
                    left[:, start - low : stop - low], right, contract, preferred_element_type=f32
                )

            update(done, done + PANEL)
            if done + PANEL < K:
                later = functools.partial(update, done + PANEL, K)


def factor_kernel(
    coarse_ref, gram_ref, prior_ref, modes_ref, upper_ref, rows_in, work, upper, inverse, out, load_sem, store_sem
):
    load = pltpu.make_async_copy(coarse_ref, rows_in, load_sem)
    load.start()
    row = lax.broadcasted_iota(jnp.int32, (K, K), 0)
    column = lax.broadcasted_iota(jnp.int32, (K, K), 1)

    def exact(left, right):
        return lax.dot_general(
            left,
            right,
            (((0,), (0,)), ((), ())),
            precision=lax.Precision.HIGHEST,
            preferred_element_type=f32,
        )

    prior_top = exact(prior_ref[:LANES, :LANES], prior_ref[:LANES, :])
    prior_low = exact(prior_ref[:, LANES:], prior_ref[:, LANES:])
    shared = gram_ref[LANES:K, :]
    turned = shared.T
    upper_half = row[:LANES, :LANES] <= column[:LANES, :LANES]
    equal = row[:LANES, :LANES] == column[:LANES, :LANES]
    work[:LANES, :LANES] = jnp.where(upper_half, shared, turned) + prior_top[:, :LANES]
    work[:LANES, LANES:K] = gram_ref[:LANES, :] + prior_top[:, LANES:]
    work[LANES:, :LANES] = jnp.zeros((LANES, LANES), f32)
    work[LANES:, LANES:K] = (
        jnp.where(equal, gram_ref[K : K + 1, :], jnp.where(upper_half, turned, shared))
        + prior_low
    )
    work[:, K:] = jnp.where(row == column, 1.0, 0.0)
    count = rows_in.shape[0]
    block = count // 4

    def give(half, rows):
        return pltpu.make_async_copy(
            out.at[half, rows], modes_ref.at[rows, pl.ds(half * LANES, LANES)], store_sem.at[half]
        )

    def halves(value):
        great, middle, _ = split(value)
        return jnp.concatenate([great, middle], axis=0)

    quarter = []

    def first_lanes(q):
        if q == 0:
            load.wait()
            quarter.append(halves(inverse[:LANES, :LANES].T))
        rows = pl.ds(q * block, block)
        part = rows_in[rows, :LANES]
        part = jnp.concatenate([part, part], axis=1)
        out[0, rows, :] = jnp.dot(part, quarter[0], preferred_element_type=f32)
        give(0, rows).start()

    factor_panels(work, upper, inverse, first_lanes)
    rest = halves(inverse[LANES:, :].T)
    for q in range(4):
        rows = pl.ds(q * block, block)
        part = rows_in[rows, :]
        part = jnp.concatenate([part, part], axis=1)
        out[1, rows, :] = jnp.dot(part, rest, preferred_element_type=f32)
        give(1, rows).start()
        if q == 0:
            upper[...] = jnp.where(row <= column, upper[...], 0.0)
            store_upper = pltpu.make_async_copy(upper, upper_ref, store_sem.at[2])
            store_upper.start()
    store_upper.wait()
    for half in range(2):
        give(half, pl.ds(0, count)).wait()


def factor_call(coarse, gram, prior):
    rows = coarse.shape[0]
    vmem = pltpu.VMEM
    return pl.pallas_call(
        factor_kernel,
        out_shape=(jax.ShapeDtypeStruct((rows, K), f32), jax.ShapeDtypeStruct((K, K), f32)),
        in_specs=[pl.BlockSpec(memory_space=pl.ANY)] + [pl.BlockSpec(memory_space=pltpu.VMEM)] * 2,
        out_specs=(pl.BlockSpec(memory_space=pl.ANY), pl.BlockSpec(memory_space=pl.ANY)),
        scratch_shapes=[
            vmem((rows, K), bf16),
            vmem((K, 2 * K), f32),
            vmem((K, K), f32),
            vmem((K, K), f32),
            vmem((2, rows, LANES), f32),
            pltpu.SemaphoreType.DMA,
            pltpu.SemaphoreType.DMA((3,)),
        ],
        compiler_params=pltpu.CompilerParams(vmem_limit_bytes=48 * 2**20),
        name="factor_and_modes",
    )(coarse, gram, prior)


def shards(snapshots, prior):
    coarse, gram = filter_call(snapshots)
    modes, upper = factor_call(coarse, gram, prior)
    return (modes.reshape(PARTS, HALF, HALF, K), upper)


def solution(mesh):
    return jax.shard_map(
        shards,
        mesh=mesh,
        in_specs=(P(None, "gx", "gy", None), P()),
        out_specs=(P(None, "gx", "gy", None), P()),
        check_vma=False,
    )
```

```python
import functools

import jax
import jax.numpy as jnp
from jax import lax
from jax.experimental import pallas as pl
from jax.experimental.pallas import tpu as pltpu
from jax.sharding import PartitionSpec as P

f32 = jnp.float32
bf16 = jnp.bfloat16
MESH = pl.DeviceIdType.MESH
TAPS = (1, 8, 28, 56, 70, 56, 28, 8, 1)
RING = 16
PARTS = 3
FINE = 64
HALF = 32
K = 256
LANES = 128
STRIP = 16
GROUP = 4
SLOTS = 40
SIDE = 4
DEEP = 8
MEMBERS = 32
PANEL = 32
OFFSETS = sorted(
    ((dx, dy, dc) for dx in range(SIDE) for dy in range(SIDE) for dc in range(2) if dx + dy + dc),
    key=lambda d: -(min(d[0], SIDE - d[0]) + min(d[1], SIDE - d[1])),
)


def tap_matrix(row_slab, cell, column_slab, y, used):
    offset = jnp.where((row_slab == column_slab) & used, y - 2 * cell + 4, -1)
    taps = jnp.zeros(offset.shape, f32)
    for place, tap in enumerate(TAPS):
        taps = jnp.where(offset == place, tap / 65536.0, taps)
    return jnp.where(row_slab % 2 == 1, 8.0 * taps, taps).astype(bf16)


def inside_taps():
    shape = (GROUP * HALF, GROUP * FINE)
    row = lax.broadcasted_iota(jnp.int32, shape, 0)
    column = lax.broadcasted_iota(jnp.int32, shape, 1)
    return tap_matrix(row // HALF, row % HALF, column // FINE, column % FINE, row >= 0)


def outside_taps():
    shape = (8 * 8, 8 * 2 * STRIP)
    row = lax.broadcasted_iota(jnp.int32, shape, 0)
    column = lax.broadcasted_iota(jnp.int32, shape, 1)
    index = row % 8
    cell = jnp.where(index < 2, index - 2, index + HALF - 2)
    along = column % (2 * STRIP)
    y = jnp.where(along < STRIP, along, along + FINE - 2 * STRIP)
    return tap_matrix(row // 8, cell, column // (2 * STRIP), y, index < 4)


def x_sum(load, cell):
    total = None

    def pair(first, second, low, high):
        have = [load(2 * q + second) for q in (low, high) if 0 <= q < HALF]
        if not have:
            return None
        value = have[0] if len(have) == 1 else have[0] + have[1]
        return value if first == 1.0 else first * value

    terms = [
        pair(1.0, 0, cell - 2, cell + 2),
        pair(28.0, 0, cell - 1, cell + 1),
        pair(70.0, 0, cell, -1),
        pair(1.0, 1, cell - 2, cell + 1),
        pair(7.0, 1, cell - 1, cell),
    ]
    for term in terms:
        if term is not None:
            total = term if total is None else total + term
    return total


def x_cell(slot):
    return slot if slot < HALF else (slot - HALF - 2 if slot < HALF + 2 else slot - 2)


def cross(left, right):
    contract = (((0,), (0,)), ((), ()))
    return lax.dot_general(left, right, contract, preferred_element_type=f32)


def cross_blocks(part):
    top = cross(part[:, :LANES], part)
    return jnp.stack([top[:, :LANES], top[:, LANES:], cross(part[:, LANES:], part[:, LANES:])])


def pack(low, mixed, high):
    row = lax.broadcasted_iota(jnp.int32, (LANES, LANES), 0)
    column = lax.broadcasted_iota(jnp.int32, (LANES, LANES), 1)
    shared = jnp.where(row <= column, low, high)
    diagonal = jnp.sum(jnp.where(row == column, high, 0.0), axis=0, keepdims=True)
    return mixed, shared, diagonal


def arrivals(ref, sem):
    pltpu.make_async_copy(ref, ref, sem).wait()


def filter_kernel(
    snap_ref,
    coarse_ref,
    gram_ref,
    tile,
    strip,
    ysum,
    yside,
    edge,
    coarse,
    rounded,
    border,
    x_out,
    x_in,
    y_out,
    y_in,
    c_stage,
    c_out,
    c_in,
    blocks,
    packed,
    rs_in,
    z_in,
    ag_in,
    load_sem,
    store_sem,
    halo_send,
    halo_recv,
    sum_send,
    sum_recv,
):
    gx = lax.axis_index("gx")
    gy = lax.axis_index("gy")
    core = lax.rem(gy, 2)
    zed = gy // 2
    gx_next, gx_last = lax.rem(gx + 1, RING), lax.rem(gx + RING - 1, RING)
    gy_next, gy_last = lax.rem(gy + 1, RING), lax.rem(gy + RING - 1, RING)

    for first in (0, FINE - GROUP):
        place = (slice(None), pl.ds(first, GROUP))
        pltpu.make_async_copy(snap_ref.at[place], tile.at[place], load_sem.at[0]).start()
    for side in range(2):
        pltpu.make_async_copy(
            snap_ref.at[:, :, pl.ds(side * (FINE - STRIP), STRIP)],
            strip.at[:, :, pl.ds(side * STRIP, STRIP)],
            load_sem.at[1],
        ).start()
    slabs = (FINE - 2 * GROUP) // 2
    loads = []
    for m in range(PARTS):
        for q in range(2):
            place = (m, pl.ds(GROUP + q * slabs, slabs))
            loads.append(
                pltpu.make_async_copy(
                    snap_ref.at[place], tile.at[place], load_sem.at[2 + len(loads)]
                )
            )
    for load in loads:
        load.start()

    barrier = pltpu.get_barrier_semaphore()

    def greet(peer):
        pl.semaphore_signal(barrier, inc=1, device_id=peer, device_id_type=MESH)

    at_x, at_y = gx // SIDE, lax.rem(gx, SIDE)
    xs = [SIDE * lax.rem(at_x + d, SIDE) for d in range(SIDE)]
    ys = [lax.rem(at_y + d, SIDE) for d in range(SIDE)]
    cores = [core, 1 - core]
    depths = [2 * lax.rem(zed + d, DEEP) + core for d in (4, 3, 5, 2, 6, 1, 7)]

    for depth in depths:
        greet((gx, depth))
    for dx, dy, dc in OFFSETS:
        greet((xs[dx] + ys[dy], 2 * zed + cores[dc]))
    for oy in (gy_last, gy_next):
        for ox in (gx_last, gx, gx_next):
            greet((ox, oy))
    for ox in (gx_last, gx_next):
        greet((ox, gy))

    def send(source, target, peer, kind):
        pltpu.make_async_remote_copy(
            src_ref=source,
            dst_ref=target,
            send_sem=halo_send.at[kind],
            recv_sem=halo_recv.at[kind],
            device_id=peer,
            device_id_type=MESH,
        ).start()

    c_stage[:, :, :, 8:, :] = jnp.zeros((2, 2, 2, 8, LANES), f32)
    taps = inside_taps()

    def y_pass(m, first):
        fine = tile[m, pl.ds(first, GROUP)].reshape(GROUP * FINE, K)
        sums = jnp.dot(taps, fine, preferred_element_type=f32)
        ysum[m, pl.ds(first, GROUP)] = sums.reshape(GROUP, HALF, K)

    arrivals(tile.at[:, pl.ds(0, 2 * GROUP)], load_sem.at[0])
    for m in range(PARTS):
        y_pass(m, 0)
        y_pass(m, FINE - GROUP)
        for side in range(2):
            for step in range(2):
                cell = (-2, HALF)[side] + step
                value = x_sum(lambda x: ysum[m, x], cell)
                x_out[side, m, step] = value.astype(bf16)

    outer = outside_taps()
    arrivals(strip, load_sem.at[1])
    for m in range(PARTS):
        for g in range(FINE // 8):
            fine = strip[m, pl.ds(g * 8, 8)].reshape(8 * 2 * STRIP, K)
            sums = jnp.dot(outer, fine, preferred_element_type=f32)
            yside[m, pl.ds(g * 8, 8)] = sums.reshape(8, 8, K)
        for slot in range(HALF + 4):
            value = x_sum(lambda x: yside[m, x], x_cell(slot))
            rows = pl.ds(m * (SLOTS * 8) + slot * 8, 8)
            edge[0, rows, :] = value[:, :LANES]
            edge[1, rows, :] = value[:, LANES:]
        for side in range(2):
            for step in range(2):
                start = m * SLOTS * 8 + side * 2 + step
                picked = [edge[h, pl.ds(start, HALF, stride=8), :] for h in range(2)]
                y_out[side, m, step] = jnp.concatenate(picked, axis=1).astype(bf16)
            for other in range(2):
                for along in range(2):
                    start = m * SLOTS * 8 + (HALF + other * 2 + along) * 8 + side * 2
                    for h in range(2):
                        c_stage[h, side, other, pl.ds((m * 2 + along) * 2, 2), :] = edge[
                            h, pl.ds(start, 2), :
                        ]

    pl.semaphore_wait(barrier, DEEP - 1 + MEMBERS - 1 + 8)
    send(x_out.at[0], x_in.at[0], (gx_last, gy), 0)
    send(x_out.at[1], x_in.at[1], (gx_next, gy), 0)
    send(y_out.at[0], y_in.at[0], (gx, gy_last), 1)
    send(y_out.at[1], y_in.at[1], (gx, gy_next), 1)
    for side, oy in ((0, gy_last), (1, gy_next)):
        for other, ox in ((0, gx_last), (1, gx_next)):
            corner = [c_stage[h, side, other] for h in range(2)]
            c_out[side, other] = jnp.concatenate(corner, axis=1).astype(bf16)
            send(c_out.at[side, other], c_in.at[side, other], (ox, oy), 2)

    along_y = lax.broadcasted_iota(jnp.int32, (16, LANES), 0)
    blocks[...] = jnp.zeros(blocks.shape, f32)
    for m in range(PARTS):
        for q in range(2):
            loads[m * 2 + q].wait()
            for g in range(slabs // GROUP):
                y_pass(m, GROUP + q * slabs + g * GROUP)

        def inside(step, carry, m=m):
            row = pl.multiple_of(step * 16, 16)
            y = along_y + row
            kept = (y >= 2) & (y < HALF - 2)
            for h in range(2):
                lanes = pl.ds(h * LANES, LANES)
                for cell in range(HALF):
                    value = x_sum(lambda x: ysum[m, x, pl.ds(row, 16), lanes], cell)
                    rows = pl.ds(pl.multiple_of(m * (HALF * HALF) + cell * HALF + row, 16), 16)
                    coarse[h, rows, :] = value
                    rounded[rows, lanes] = jnp.where(kept, value, 0.0).astype(bf16)
            return carry

        lax.fori_loop(0, 2, inside, 0)
        rows = pl.ds(m * HALF * HALF + 2 * HALF, (HALF - 4) * HALF)
        blocks[...] += cross_blocks(rounded[rows, :])

    for kind, arrived in enumerate((x_in, y_in, c_in)):
        arrivals(arrived, halo_recv.at[kind])
    for m in range(PARTS):
        for side in range(2):
            for step in range(2):
                cell = (HALF - 2, 0)[side] + step
                rows = pl.ds(m * HALF * HALF + cell * HALF, HALF)
                value = x_in[side, m, step].astype(f32)
                for h in range(2):
                    coarse[h, rows, :] += value[:, h * LANES : (h + 1) * LANES]
    for side in range(2):
        for other in range(2):
            corner = c_in[side, other].astype(f32)
            for m in range(PARTS):
                for along in range(2):
                    row = (HALF - 2, 0)[other] + along
                    column = (HALF - 2, 0)[side]
                    source = (m * 2 + along) * 2
                    target = pl.ds(m * HALF * HALF + row * HALF + column, 2)
                    value = corner[source : source + 2, :]
                    for h in range(2):
                        coarse[h, target, :] += value[:, h * LANES : (h + 1) * LANES]
    along_x = lax.broadcasted_iota(jnp.int32, (HALF, LANES), 0)
    kept = (along_x >= 2) & (along_x < HALF - 2)
    for m in range(PARTS):
        for side in range(2):
            for step in range(2):
                cell = (HALF - 2, 0)[side] + step
                rows = pl.ds(m * HALF * HALF + cell, HALF, stride=HALF)
                value = y_in[side, m, step].astype(f32)
                place = pl.ds(((m * 2 + side) * 2 + step) * HALF, HALF)
                for h in range(2):
                    total = coarse[h, rows, :] + value[:, h * LANES : (h + 1) * LANES]
                    coarse[h, rows, :] = total
                    border[place, pl.ds(h * LANES, LANES)] = jnp.where(kept, total, 0.0).astype(
                        bf16
                    )
    for m in range(PARTS):
        for side in range(2):
            rows = pl.ds(m * HALF * HALF + (HALF - 2, 0)[side] * HALF, 2 * HALF)
            place = pl.ds((PARTS * 4 + (m * 2 + side) * 2) * HALF, 2 * HALF)
            for h in range(2):
                border[place, pl.ds(h * LANES, LANES)] = coarse[h, rows, :].astype(bf16)

    total = blocks[...]
    half_border = PARTS * 4 * HALF
    for part in range(2):
        total += cross_blocks(border[pl.ds(part * half_border, half_border), :])
    mixed, shared, diagonal = pack(total[0], total[1], total[2])
    packed[0 : LANES // 8, 0:8, :] = mixed.reshape(LANES // 8, 8, LANES)
    packed[LANES // 8 :, 0:8, :] = shared.reshape(LANES // 8, 8, LANES)
    packed[:, 8:9, :] = jnp.broadcast_to(diagonal[None], (MEMBERS, 1, LANES))

    me = gx * 2 + core

    def to_members(source_of, target, phase):
        for dx, dy, dc in OFFSETS:
            peer = xs[dx] + ys[dy]
            pltpu.make_async_remote_copy(
                src_ref=source_of(peer * 2 + cores[dc]),
                dst_ref=target.at[me],
                send_sem=sum_send.at[phase],
                recv_sem=sum_recv.at[phase],
                device_id=(peer, 2 * zed + cores[dc]),
                device_id_type=MESH,
            ).start()

    def sum_slots(slots, count):
        total = slots[0]
        for slot in range(1, count):
            total = total + slots[slot]
        return total

    to_members(lambda other: packed.at[other], rs_in, 0)
    rs_in[me] = packed[me]

    block = 512

    def finish(step, carry):
        rows = pl.ds(pl.multiple_of(step * block, block), block)
        for h in range(2):
            rounded[rows, pl.ds(h * LANES, LANES)] = coarse[h, rows, :].astype(bf16)
        return carry

    lax.fori_loop(0, PARTS * HALF * HALF // block, finish, 0)
    store = pltpu.make_async_copy(rounded, coarse_ref, store_sem)
    store.start()
    arrivals(rs_in.at[pl.ds(0, MEMBERS - 1)], sum_recv.at[0])

    z_in[zed] = sum_slots(rs_in, MEMBERS)
    for depth in depths:
        pltpu.make_async_remote_copy(
            src_ref=z_in.at[zed],
            dst_ref=z_in.at[zed],
            send_sem=sum_send.at[1],
            recv_sem=sum_recv.at[1],
            device_id=(gx, depth),
            device_id_type=MESH,
        ).start()
    arrivals(z_in.at[pl.ds(0, DEEP - 1)], sum_recv.at[1])

    ag_in[me] = sum_slots(z_in, DEEP)
    to_members(lambda other: ag_in.at[me], ag_in, 2)
    arrivals(ag_in.at[pl.ds(0, MEMBERS - 1)], sum_recv.at[2])

    count = PARTS * HALF * HALF * RING * RING
    share = 1.0 / count
    gram_ref[:K, :] = ag_in[:, 0:8, :].reshape(K, LANES) * share
    gram_ref[K:, :] = jnp.broadcast_to(ag_in[0, 8:9, :] * share, (8, LANES))
    for kind, sent in enumerate((x_out, y_out, c_out)):
        arrivals(sent, halo_send.at[kind])
    arrivals(packed.at[pl.ds(0, MEMBERS - 1)], sum_send.at[0])
    arrivals(z_in.at[pl.ds(0, DEEP - 1)], sum_send.at[1])
    arrivals(ag_in.at[pl.ds(0, MEMBERS - 1)], sum_send.at[2])
    store.wait()


def filter_call(snapshots):
    rows = PARTS * HALF * HALF
    vmem = pltpu.VMEM
    dma = pltpu.SemaphoreType.DMA
    return pl.pallas_call(
        filter_kernel,
        out_shape=(
            jax.ShapeDtypeStruct((rows, K), bf16),
            jax.ShapeDtypeStruct((K + 8, LANES), f32),
        ),
        in_specs=[pl.BlockSpec(memory_space=pltpu.HBM)],
        out_specs=(pl.BlockSpec(memory_space=pl.ANY), pl.BlockSpec(memory_space=pltpu.VMEM)),
        scratch_shapes=[
            vmem((PARTS, FINE, FINE, K), bf16),
            vmem((PARTS, FINE, 2 * STRIP, K), bf16),
            vmem((PARTS, FINE, HALF, K), f32),
            vmem((PARTS, FINE, 8, K), f32),
            vmem((2, PARTS * SLOTS * 8, LANES), f32),
            vmem((2, rows, LANES), f32),
            vmem((rows, K), bf16),
            vmem((PARTS * 8 * HALF, K), bf16),
            vmem((2, PARTS, 2, HALF, K), bf16),
            vmem((2, PARTS, 2, HALF, K), bf16),
            vmem((2, PARTS, 2, HALF, K), bf16),
            vmem((2, PARTS, 2, HALF, K), bf16),
            vmem((2, 2, 2, 16, LANES), f32),
            vmem((2, 2, 16, K), bf16),
            vmem((2, 2, 16, K), bf16),
            vmem((3, LANES, LANES), f32),
            vmem((MEMBERS, 9, LANES), f32),
            vmem((MEMBERS, 9, LANES), f32),
            vmem((DEEP, 9, LANES), f32),
            vmem((MEMBERS, 9, LANES), f32),
            dma((2 + PARTS * 2,)),
            dma,
            dma((3,)),
            dma((3,)),
            dma((3,)),
            dma((3,)),
        ],
        compiler_params=pltpu.CompilerParams(
            collective_id=0, has_side_effects=True, vmem_limit_bytes=48 * 2**20
        ),
        name="filter_and_gram",
    )(snapshots)


def split(value):
    high = value.astype(bf16)
    rest = value - high.astype(f32)
    middle = rest.astype(bf16)
    return high, middle, (rest - middle.astype(f32)).astype(bf16)


def factor_panels(work, upper, inverse, beside):
    place = lax.broadcasted_iota(jnp.int32, (8, LANES), 0)
    parts = PANEL // 8
    contract = (((0,), (0,)), ((), ()))

    def spread(value, row):
        return jnp.broadcast_to(value[row : row + 1, :], (8, LANES))

    later = None
    for first in range(0, K, PANEL):
        rows = pl.ds(first, PANEL)
        low = 0 if first < LANES else LANES
        high = low + 3 * LANES
        strip = work[rows, low:high]
        columns = [
            [
                jnp.broadcast_to(
                    strip[8 * t : 8 * t + 8, first - low + k : first - low + k + 1], (8, LANES)
                )
                if t >= k // 8
                else None
                for t in range(parts)
            ]
            for k in range(PANEL)
        ]
        tiles = [
            [strip[8 * t : 8 * t + 8, q * LANES : (q + 1) * LANES] for q in range(3)]
            for t in range(parts)
        ]
        pivots = [None] * parts
        pivot = spread(columns[0][0], 0)
        for j in range(PANEL):
            top, row = divmod(j, 8)
            column = columns[j]
            pivots[top] = pivot if row == 0 else jnp.where(place == row, pivot, pivots[top])
            if j == PANEL - 1:
                break
            if j == 2 and later is not None:
                later()
                later = None
            if j == 6 and first >= LANES:
                beside((first - LANES) // PANEL)
            over = 1.0 / pivot
            nearby = spread(column[(j + 1) // 8], (j + 1) % 8)
            pivot = spread(columns[j + 1][(j + 1) // 8], (j + 1) % 8) - (nearby * nearby) * over
            factor = {}
            for t in range(top if row < 7 else top + 1, parts):
                value = column[t] * over
                factor[t] = jnp.where(place > row, value, 0.0) if t == top else value
            for k in range(j + 1, PANEL):
                across = spread(column[k // 8], k % 8)
                for t in range(k // 8, parts):
                    columns[k][t] = columns[k][t] - factor[t] * across
            source = [spread(value, row) for value in tiles[top]]
            for t in factor:
                tiles[t] = [tiles[t][q] - factor[t] * source[q] for q in range(3)]
        strip = jnp.concatenate(
            [
                jnp.concatenate([value * lax.rsqrt(pivots[t]) for value in tiles[t]], axis=1)
                for t in range(parts)
            ],
            axis=0,
        )
        if low == 0:
            upper[rows, :] = strip[:, :K]
            inverse[rows, :LANES] = strip[:, K:]
            inverse[rows, LANES:] = jnp.zeros((PANEL, LANES), f32)
        else:
            upper[rows, :LANES] = jnp.zeros((PANEL, LANES), f32)
            upper[rows, LANES:] = strip[:, :LANES]
            inverse[rows, :] = strip[:, LANES:]
        done = first + PANEL
        if done < K:
            great, middle, small = split(strip)
            left = jnp.concatenate([great, great, middle, great, small, middle], axis=0)
            right = jnp.concatenate([great, middle, great, small, great, middle], axis=0)

            def update(start, stop, left=left, right=right, low=low, high=high):
                work[start:stop, low:high] -= lax.dot_general(
                    left[:, start - low : stop - low], right, contract, preferred_element_type=f32
                )

            update(done, done + PANEL)
            if done + PANEL < K:
                later = functools.partial(update, done + PANEL, K)


def factor_kernel(
    coarse_ref, gram_ref, prior_ref, modes_ref, upper_ref, rows_in, work, upper, inverse, out, load_sem, store_sem
):
    load = pltpu.make_async_copy(coarse_ref, rows_in, load_sem)
    load.start()
    row = lax.broadcasted_iota(jnp.int32, (K, K), 0)
    column = lax.broadcasted_iota(jnp.int32, (K, K), 1)

    def exact(left, right):
        return lax.dot_general(
            left,
            right,
            (((0,), (0,)), ((), ())),
            precision=lax.Precision.HIGHEST,
            preferred_element_type=f32,
        )

    prior_top = exact(prior_ref[:LANES, :LANES], prior_ref[:LANES, :])
    prior_low = exact(prior_ref[:, LANES:], prior_ref[:, LANES:])
    shared = gram_ref[LANES:K, :]
    turned = shared.T
    upper_half = row[:LANES, :LANES] <= column[:LANES, :LANES]
    equal = row[:LANES, :LANES] == column[:LANES, :LANES]
    work[:LANES, :LANES] = jnp.where(upper_half, shared, turned) + prior_top[:, :LANES]
    work[:LANES, LANES:K] = gram_ref[:LANES, :] + prior_top[:, LANES:]
    work[LANES:, :LANES] = jnp.zeros((LANES, LANES), f32)
    work[LANES:, LANES:K] = (
        jnp.where(equal, gram_ref[K : K + 1, :], jnp.where(upper_half, turned, shared))
        + prior_low
    )
    work[:, K:] = jnp.where(row == column, 1.0, 0.0)
    count = rows_in.shape[0]
    block = count // 4

    def give(half, rows):
        return pltpu.make_async_copy(
            out.at[half, rows], modes_ref.at[rows, pl.ds(half * LANES, LANES)], store_sem.at[half]
        )

    def halves(value):
        great, middle, _ = split(value)
        return jnp.concatenate([great, middle], axis=0)

    quarter = []

    def first_lanes(q):
        if q == 0:
            load.wait()
            quarter.append(halves(inverse[:LANES, :LANES].T))
        rows = pl.ds(q * block, block)
        part = rows_in[rows, :LANES]
        part = jnp.concatenate([part, part], axis=1)
        out[0, rows, :] = jnp.dot(part, quarter[0], preferred_element_type=f32)
        give(0, rows).start()

    factor_panels(work, upper, inverse, first_lanes)
    rest = halves(inverse[LANES:, :].T)
    for q in range(4):
        rows = pl.ds(q * block, block)
        part = rows_in[rows, :]
        part = jnp.concatenate([part, part], axis=1)
        out[1, rows, :] = jnp.dot(part, rest, preferred_element_type=f32)
        give(1, rows).start()
        if q == 0:
            upper[...] = jnp.where(row <= column, upper[...], 0.0)
            store_upper = pltpu.make_async_copy(upper, upper_ref, store_sem.at[2])
            store_upper.start()
    store_upper.wait()
    for half in range(2):
        give(half, pl.ds(0, count)).wait()


def factor_call(coarse, gram, prior):
    rows = coarse.shape[0]
    vmem = pltpu.VMEM
    return pl.pallas_call(
        factor_kernel,
        out_shape=(jax.ShapeDtypeStruct((rows, K), f32), jax.ShapeDtypeStruct((K, K), f32)),
        in_specs=[pl.BlockSpec(memory_space=pl.ANY)] + [pl.BlockSpec(memory_space=pltpu.VMEM)] * 2,
        out_specs=(pl.BlockSpec(memory_space=pl.ANY), pl.BlockSpec(memory_space=pl.ANY)),
        scratch_shapes=[
            vmem((rows, K), bf16),
            vmem((K, 2 * K), f32),
            vmem((K, K), f32),
            vmem((K, K), f32),
            vmem((2, rows, LANES), f32),
            pltpu.SemaphoreType.DMA,
            pltpu.SemaphoreType.DMA((3,)),
        ],
        compiler_params=pltpu.CompilerParams(vmem_limit_bytes=48 * 2**20),
        name="factor_and_modes",
    )(coarse, gram, prior)


def shards(snapshots, prior):
    coarse, gram = filter_call(snapshots)
    modes, upper = factor_call(coarse, gram, prior)
    return (modes.reshape(PARTS, HALF, HALF, K), upper)


def solution(mesh):
    return jax.shard_map(
        shards,
        mesh=mesh,
        in_specs=(P(None, "gx", "gy", None), P()),
        out_specs=(P(None, "gx", "gy", None), P()),
        check_vma=False,
    )
```
